32 devices in a mesh: dp: 8 (over y, x, core), expert: 4 (over z).
Axes of the slice: x: 2, y: 2, z: 4, core: 2. Of those that a mesh axis runs over, the one named last changes fastest.
Arguments:
- hidden_in: bfloat16 [128, 4096], P(('dp', 'expert')), may hold values from -6 to 6
- norm_gain: bfloat16 [4096], replicated, may hold values from 0.099609375 to 1.8984375
- expert_ids: int32 [128, 8], P(('dp', 'expert')), may hold values from 0 to 63, all different within a row; in each aligned block of 16 rows (0 to 15, 16 to 31, ...) at most 4 rows name the same one
- gate_share: bfloat16 [128, 8], P(('dp', 'expert')), may hold values from 0.049804688 to 0.25
- w_gate: bfloat16 [512, 192, 4096], P(('dp', 'expert')), may hold values from -0.09375 to 0.09375
- w_up: bfloat16 [512, 192, 4096], P(('dp', 'expert')), may hold values from -0.09375 to 0.09375
- w_down: bfloat16 [512, 192, 4096], P(('dp', 'expert')), may hold values from -0.15625 to 0.15625
Outputs:
- layer_out: bfloat16 [128, 4096], P(('dp', 'expert'))
The draws below stay inside these ranges and needn't reach their ends.
Inputs may be any that keep to these rules, and one draw needn't show every extreme that they name: `expert_ids`: each row names 8 different experts. Among the 16 rows of one request group (aligned blocks of 16 rows), no expert is named by more than 4 rows.
All inputs are finite; a program needn't handle non-finite values.
Results may differ from the reference program's by a relative error of at most 0.01.
Values may be sent and summed in bfloat16 or wider, within the bound.
A program may use at most 128 MiB of HBM per device.

```python
import math
import jax
import jax.numpy as jnp
import numpy as np
from jax import lax

D = 4096
FF = 1536
TOP = 8
EXPERTS = 64
SPLIT = 8
FF_DEV = 192
TOK_ROW = 16
TOKENS = 128
CAP = 4
SLOTS = 512
GROUP = 8
N_DP = 8


def block_levels(key, shape, shards, low, high):
    factor_of = 1.0
    for axis_at, blocks in shards:
        steps = jax.random.uniform(jax.random.fold_in(jax.random.fold_in(key, 6), axis_at), (blocks,), jnp.float32, low / len(shards), high / len(shards))
        factor_of = factor_of * jnp.repeat(jnp.exp(steps), shape[axis_at] // blocks).reshape((-1,) + (1,) * (len(shape) - 1 - axis_at))
    return factor_of


def routed_block(own_key, own, number, rows, number_of, top, bound, skew):
    ranking = jax.random.permutation(own_key, number_of)
    packed, common = load_shares(number_of, rows * top, bound, skew, True), load_shares(number_of, rows * top, bound, skew, False)
    places = jnp.arange(number_of)

    def named(tallies, offset_by):
        used = int((tallies > 0).sum())
        fixed = max(1, used // 4)
        moved = fixed + (places - fixed + offset_by * (used - fixed)) % max(1, number_of - fixed)
        return jnp.zeros((number_of,), jnp.int32).at[ranking[jnp.where(places < fixed, places, moved)]].set(jnp.asarray(tallies, jnp.int32))

    tallies = jnp.where(number % 4 == 0, named(packed, number // 4), named(common, number - number // 4 - 1))
    mixed = jax.random.permutation(jax.random.fold_in(own, 3), number_of)
    giver, taker = mixed[0:number_of // 2 * 2:2], mixed[1:number_of // 2 * 2:2]
    slack = jnp.minimum(tallies[giver] - 1, bound - tallies[taker]) // 2
    slack = jnp.where((giver == ranking[0]) | (taker == ranking[0]) | (tallies[taker] == 0), 0, jnp.maximum(slack, 0))
    moved = jax.random.randint(jax.random.fold_in(own, 4), (number_of // 2,), 0, 1 << 20) % (slack + 1)
    tallies = tallies.at[giver].add(-moved).at[taker].add(moved)
    labels = jnp.searchsorted(jnp.cumsum(tallies), jnp.arange(rows * top), side="right").astype(jnp.int32)
    table = labels.reshape(top, rows).T
    table = table[jax.random.permutation(jax.random.fold_in(own, 1), rows)]
    offset_by = jax.random.randint(jax.random.fold_in(own, 2), (rows, 1), 0, top)
    return jnp.take_along_axis(table, (jnp.arange(top)[None, :] + offset_by) % top, axis=1)


def load_shares(number_of, total, most, skew, full):
    portions = [(1 << 20) // math.isqrt(rank ** skew) + 1 for rank in range(1, number_of + 1)]
    largest = most if full else min(most, max(-(-total // number_of), total * portions[0] // sum(portions)))
    least = 1 if total - largest >= number_of - 1 else 0
    counts, spare = [largest] + [least] * (number_of - 1), total - largest - least * (number_of - 1)
    while spare > 0:
        movable = [i for i in range(1, number_of) if counts[i] < largest] or [i for i in range(1, number_of) if counts[i] < most]
        mass, remaining = sum([portions[i] for i in movable]), spare
        for i in movable:
            more = min(most - counts[i], max(1, remaining * portions[i] // mass), spare)
            counts[i] = counts[i] + more
            spare = spare - more
    return np.array(counts)


def gaussian(rng, shape, spread, reach, pieces=(), held_as=jnp.bfloat16):
    result = spread * jax.random.normal(rng, shape, jnp.float32)
    if pieces:
        result = result * block_levels(rng, shape, pieces, -0.22, 0.18)
    return jnp.clip(result, -reach, reach).astype(held_as)


def setup_inputs(seed: int = 0) -> dict:
    splits = jax.random.split(jax.random.key(seed), 8)
    hidden_in = gaussian(splits[0], (TOKENS, D), 1.0, 6.0, ((0, 32),))
    norm_gain = jnp.clip(1.0 + 0.18 * jax.random.normal(splits[1], (D,), jnp.float32), 0.099609375, 1.8984375).astype(jnp.bfloat16)
    expert_ids_keys = jax.random.split(jax.random.fold_in(splits[2], 1), TOKENS // TOK_ROW)
    expert_ids_turns = jax.random.permutation(jax.random.fold_in(splits[2], 3), TOKENS // TOK_ROW)
    expert_ids = jax.vmap(lambda own, number: routed_block(jax.random.fold_in(splits[2], 2), own, number, TOK_ROW, EXPERTS, TOP, CAP, 1))(expert_ids_keys, expert_ids_turns).reshape((TOKENS, TOP))
    gate_share = jnp.clip(0.049804688 + 0.20019531 * jax.random.uniform(splits[3], (TOKENS, TOP), jnp.float32) ** block_levels(splits[3], (TOKENS, TOP), ((0, 32),), -0.2, 0.2), 0.049804688, 0.25).astype(jnp.bfloat16)
    w_gate = gaussian(splits[4], (SLOTS, FF_DEV, D), D ** -0.5, 0.09375, ((0, 32),))
    w_up = gaussian(splits[5], (SLOTS, FF_DEV, D), D ** -0.5, 0.09375, ((0, 32),))
    w_down = gaussian(splits[6], (SLOTS, FF_DEV, D), FF ** -0.5, 0.15625, ((0, 32),))
    return {"hidden_in": hidden_in, "norm_gain": norm_gain, "expert_ids": expert_ids, "gate_share": gate_share, "w_gate": w_gate, "w_up": w_up, "w_down": w_down}


def expert_rows(row_block, gate_w, up_w, down_w):
    row_f = row_block.astype(jnp.float32)
    gate_vals = jnp.einsum('rd,sfd->rsf', row_f, gate_w.astype(jnp.float32))
    up_vals = jnp.einsum('rd,sfd->rsf', row_f, up_w.astype(jnp.float32))
    activated = lax.optimization_barrier((jax.nn.silu(gate_vals) * up_vals).astype(jnp.bfloat16))
    projected = jnp.einsum('rsf,sfd->rsd', activated.astype(jnp.float32), down_w.astype(jnp.float32))
    grouped = lax.optimization_barrier(jnp.sum(projected.reshape(projected.shape[0], SPLIT // GROUP, GROUP, D), axis=2))
    rounded = lax.optimization_barrier(grouped.astype(jnp.bfloat16))
    return lax.optimization_barrier(jnp.sum(rounded.astype(jnp.float32), axis=1))

def reference(hidden_in, norm_gain, expert_ids, gate_share, w_gate, w_up, w_down):
    resid = hidden_in.astype(jnp.float32)
    inv_rms = lax.rsqrt(lax.optimization_barrier(jnp.mean(resid * resid, axis=1, keepdims=True)) + 1e-06)
    normed = (resid * inv_rms * norm_gain.astype(jnp.float32)[None, :]).astype(jnp.bfloat16)
    flat_ids = expert_ids.reshape(-1).astype(jnp.int32)
    onehot = (flat_ids[:, None] == jnp.arange(EXPERTS, dtype=jnp.int32)[None, :]).astype(jnp.int32)
    order_pos = lax.optimization_barrier(jnp.sum((jnp.cumsum(onehot, axis=0) - onehot) * onehot, axis=1)).astype(jnp.int32)
    per_expert = N_DP * CAP
    slot_index = (flat_ids * per_expert + order_pos).astype(jnp.int32)
    token_of = (jnp.arange(TOKENS * TOP, dtype=jnp.int32) // TOP).astype(jnp.int32)
    row_table = jnp.full((EXPERTS * per_expert,), TOKENS, dtype=jnp.int32).at[slot_index].set(token_of)
    padded = jnp.concatenate([normed, jnp.zeros((1, D), jnp.bfloat16)], axis=0)
    gate_all = w_gate.reshape(EXPERTS, SPLIT, FF_DEV, D)
    up_all = w_up.reshape(EXPERTS, SPLIT, FF_DEV, D)
    down_all = w_down.reshape(EXPERTS, SPLIT, FF_DEV, D)

    def one_expert(items):
        index_rows, gate_w, up_w, down_w = items
        return expert_rows(padded[index_rows], gate_w, up_w, down_w)
    expert_out = lax.map(one_expert, (row_table.reshape(EXPERTS, per_expert), gate_all, up_all, down_all))
    picked = expert_out.reshape(EXPERTS * per_expert, D)[slot_index].reshape(TOKENS, TOP, D)
    routed = lax.optimization_barrier(jnp.sum(picked * gate_share.astype(jnp.float32)[:, :, None], axis=1))
    return (resid + routed).astype(jnp.bfloat16)
```

```python
import functools

import jax
import jax.numpy as jnp
from jax import lax
from jax.experimental import pallas as pl
from jax.experimental.pallas import tpu as pltpu
from jax.sharding import PartitionSpec as P

EXPERTS = 64
SPLIT = 8

ROWS = 16
QUART = 4
META = 128
PAIRS = 5
MESH = pl.DeviceIdType.MESH
BF = jnp.bfloat16
F32 = jnp.float32


def iota(shape, dim):
    return lax.broadcasted_iota(jnp.int32, shape, dim)


def dot(a, b):
    return jnp.dot(a, b, preferred_element_type=F32)


def dot_nt(a, b):
    return lax.dot_general(a, b, (((1,), (1,)), ((), ())), preferred_element_type=F32)


def tok_of(r):
    return (r // ROWS) % QUART * 4 + r % 4


def quarter_of(r):
    return r % ROWS // 4


def moe_kernel(
    n_dp, n_z, n_exp, chunk, n_gu, n_j,
    hid_ref, gain_ref, ids_ref, share_ref, wg, wu, wd,
    out_ref,
    buf, xs, gbuf, ubuf, dbuf, act, pay, ob_send, ob_recv, z_send, z_recv, z_own, fin, wmat,
    g_sem, u_sem, d_sem,
    zs_s, zs_r, xy_s, xy_r, co_s, co_r, fw_s, fw_r, ob_s, ob_r, zz_s, zz_r,
):
    dp = lax.axis_index("dp")
    z = lax.axis_index("expert")
    d_model = hid_ref.shape[1]
    ff = n_gu * chunk
    quarter = d_model // QUART
    j_cols = d_model // n_j
    j_quart = j_cols // QUART
    cap_rows = n_dp * 4
    n_rows = n_dp * n_z * ROWS

    def gu_copies(p):
        slot = lax.rem(p, PAIRS)
        rows = pl.ds(pl.multiple_of(p * chunk, chunk), chunk)
        return (
            pltpu.make_async_copy(wg.at[rows], gbuf.at[slot], g_sem.at[slot]),
            pltpu.make_async_copy(wu.at[rows], ubuf.at[slot], u_sem.at[slot]),
        )

    def d_copy(i, j):
        return pltpu.make_async_copy(
            wd.at[
                pl.ds(pl.multiple_of(i * ff, ff), ff),
                pl.ds(pl.multiple_of(j * j_cols, j_cols), j_cols),
            ],
            dbuf.at[j],
            d_sem.at[j],
        )

    def start_gu(p):
        a, b = gu_copies(p)
        a.start()
        b.start()

    n_pairs = n_exp * n_gu
    for p in range(n_gu):
        start_gu(jnp.int32(p))
    for j in range(n_j):
        d_copy(jnp.int32(0), jnp.int32(j)).start()
    for p in range(n_gu, min(PAIRS, n_pairs)):
        start_gu(jnp.int32(p))

    core = lax.rem(dp, 2)
    xc = lax.rem(lax.div(dp, 2), 2)
    yc = lax.div(dp, 4)
    flip_c = 1 - 2 * core
    flip_x = 2 - 4 * xc
    flip_y = 4 - 8 * yc
    sib = dp + flip_c
    flips = (flip_x, flip_y, flip_x + flip_y)
    barrier = pltpu.get_barrier_semaphore()
    for k in range(1, n_dp):
        pl.semaphore_signal(
            barrier, inc=1, device_id=(lax.rem(dp + k, n_dp), z), device_id_type=MESH
        )
    for k in range(1, n_z):
        pl.semaphore_signal(
            barrier, inc=1, device_id=(dp, lax.rem(z + k, n_z)), device_id_type=MESH
        )

    resid = hid_ref[...].astype(F32)
    inv_rms = lax.rsqrt(jnp.mean(resid * resid, axis=1, keepdims=True) + 1e-06)
    normed = resid * inv_rms * gain_ref[...].astype(F32)
    put = iota((8, META), 1) - iota((8, META), 0)
    meta = dot(ids_ref[...].astype(F32).astype(BF), (put == 0).astype(F32).astype(BF)) + dot(
        share_ref[...], (put == 8).astype(F32).astype(BF)
    )
    for j in range(QUART):
        pay[4 * j : 4 * j + 4, 0:quarter] = normed[:, j * quarter : (j + 1) * quarter]
        pay[4 * j : 4 * j + 4, quarter : quarter + META] = meta
    me = dp * n_z + z
    buf[me] = pay[...].astype(BF)

    pl.semaphore_wait(barrier, n_dp - 1 + n_z - 1)

    def remote(src, dst, s, r, to):
        return pltpu.make_async_remote_copy(
            src_ref=src, dst_ref=dst, send_sem=s, recv_sem=r, device_id=to, device_id_type=MESH
        )

    def z_copy(k):
        blk = buf.at[me]
        return remote(blk, blk, zs_s.at[k - 1], zs_r.at[k - 1], (dp, lax.rem(z + k, n_z)))

    def xy_copy(f, k, zb):
        blk = buf.at[dp * n_z + zb]
        return remote(blk, blk, xy_s.at[f, k], xy_r.at[f, k], (dp + flips[f], z))

    def co_copy(k, zb):
        blk = buf.at[dp * n_z + zb]
        return remote(blk, blk, co_s.at[k], co_r.at[k], (sib, z))

    def fw_copy(f):
        blk = buf.at[pl.ds((dp + flips[f]) * n_z, n_z)]
        return remote(blk, blk, fw_s.at[f], fw_r.at[f], (sib, z))

    for k in range(1, n_z):
        z_copy(k).start()
    for k in range(n_z):
        zb = lax.rem(z + n_z - k, n_z)
        if k > 0:
            z_copy(k).wait_recv()
        for f in range(3):
            xy_copy(f, k, zb).start()
        co_copy(k, zb).start()

    tr, tc = iota((n_rows, 1), 0), iota((1, n_rows), 1)
    before = (
        (tr // (n_z * ROWS) == tc // (n_z * ROWS))
        & (quarter_of(tr) == 0)
        & (tok_of(tr) < tok_of(tc))
    )
    before = before.astype(F32).astype(BF)

    for f in range(3):
        for k in range(n_z):
            xy_copy(f, k, z).wait_recv()
        fw_copy(f).start()
    for k in range(n_z):
        co_copy(k, z).wait_recv()
    for f in range(3):
        fw_copy(f).wait_recv()

    meta_all = buf[:, :, quarter : quarter + META].reshape(n_rows, META)
    pick = (iota((16, META), 0) == iota((16, META), 1)).astype(F32).astype(BF)
    meta_t = dot_nt(pick, meta_all)
    ids_t = meta_t[0:8]
    first = (me * n_exp).astype(F32)
    lane_q = quarter_of(tc)
    group = (tc // (n_z * ROWS) * 4).astype(F32)
    slot_iota = iota((cap_rows, 1), 0).astype(F32)
    for i in range(n_exp):
        hit = jnp.sum((ids_t == first + i).astype(F32), axis=0, keepdims=True)
        rank = dot(jnp.broadcast_to(hit, (8, n_rows)).astype(BF), before)[0:1]
        key = jnp.where(hit > 0, group + rank, -1.0)
        for j in range(QUART):
            key_j = jnp.where(lane_q == j, key, -1.0)
            sel = (slot_iota == key_j).astype(F32).astype(BF)
            xs[i, :, j * quarter : (j + 1) * quarter] = dot(
                sel, buf[:, :, 0:quarter].reshape(n_rows, quarter)
            ).astype(BF)

    grp = n_z * ROWS
    meta_g = buf[pl.ds(dp * n_z, n_z), :, quarter : quarter + META].reshape(grp, META).astype(F32)
    gr, gc = iota((grp, 1), 0), iota((1, grp), 1)
    before_g = ((quarter_of(gc) == 0) & (tok_of(gc) < tok_of(gr))).astype(F32).astype(BF)
    lanes = n_dp * ROWS
    lc = iota((1, lanes), 1)
    lane_first = ((lc // ROWS * n_z + z) * n_exp).astype(F32)
    same_q = quarter_of(gr) == quarter_of(lc)
    lane_slot = (lc % 4).astype(F32)
    for i in range(n_exp):
        hits = jnp.zeros((grp, lanes), F32)
        shares = jnp.zeros((grp, lanes), F32)
        for k in range(8):
            match = meta_g[:, k : k + 1] == lane_first + i
            hits = hits + match.astype(F32)
            shares = shares + jnp.where(match, meta_g[:, 8 + k : 9 + k], 0.0)
        rank = dot(before_g, hits.astype(BF))
        keep = (hits > 0) & (rank == lane_slot) & same_q
        wmat[i] = jnp.where(keep, shares, 0.0).astype(BF)

    def ob_copy(i, j, k):
        to = lax.rem(dp + k, n_dp)
        return remote(
            ob_send.at[i, j, to], ob_recv.at[i, j, dp], ob_s.at[i, j, k - 1],
            ob_r.at[i, j, k - 1], (to, z),
        )

    pr, pc = iota((lanes, 1), 0), iota((1, cap_rows), 1)
    same_slot = pr // ROWS * 4 + pr % 4 == pc
    spread = [
        (same_slot & (quarter_of(pr) == q)).astype(F32).astype(BF) for q in range(QUART)
    ]

    def expert(i, carry):
        def gu_step(c, carry):
            p = i * n_gu + c
            slot = lax.rem(p, PAIRS)
            a, b = gu_copies(p)
            a.wait()
            gate = dot_nt(xs[i], gbuf[slot])
            b.wait()
            up = dot_nt(xs[i], ubuf[slot])
            act[c] = (gate / (1.0 + jnp.exp(-gate)) * up).astype(BF)

            @pl.when(p + PAIRS < n_pairs)
            def _():
                start_gu(p + PAIRS)

            return carry

        lax.fori_loop(0, n_gu, gu_step, 0)

        def d_step(j, carry):
            d_copy(i, j).wait()
            total = dot(act[0], dbuf[j, 0:chunk, :])
            for c in range(1, n_gu):
                total = total + dot(act[c], dbuf[j, c * chunk : (c + 1) * chunk, :])
            total = total.astype(BF)

            @pl.when(i + 1 < n_exp)
            def _():
                d_copy(i + 1, j).start()

            rows = dot(spread[0], total[:, 0:j_quart])
            for q in range(1, QUART):
                rows = rows + dot(spread[q], total[:, q * j_quart : (q + 1) * j_quart])
            ob_send[i, j] = rows.astype(BF).reshape(n_dp, ROWS, j_quart)
            for k in range(1, n_dp):
                ob_copy(i, j, k).start()
            ob_recv[i, j, dp] = ob_send[i, j, dp]
            return carry

        lax.fori_loop(0, n_j, d_step, 0)
        return carry

    lax.fori_loop(0, n_exp, expert, 0)

    def zz_copy(j, k):
        to = lax.rem(z + k, n_z)
        return remote(
            z_send.at[j, to], z_recv.at[j, z], zz_s.at[j, k - 1], zz_r.at[j, k - 1], (dp, to)
        )

    for j in range(n_j):
        part = jnp.zeros((grp, j_quart), F32)
        for i in range(n_exp):
            for k in range(1, n_dp):
                ob_copy(i, j, k).wait_recv()
            part = part + dot(wmat[i], ob_recv[i, j].reshape(lanes, j_quart))
        z_send[j] = part.astype(BF).reshape(n_z, ROWS, j_quart)
        z_own[j] = part.reshape(n_z, ROWS, j_quart)
        for k in range(1, n_z):
            zz_copy(j, k).start()
    for j in range(n_j):
        total = z_own[j, z]
        for k in range(1, n_z):
            zz_copy(j, k).wait_recv()
            total = total + z_recv[j, lax.rem(z + n_z - k, n_z)].astype(F32)
        fin[j] = total
        for q in range(QUART):
            at = j * j_cols + q * j_quart
            out_ref[:, at : at + j_quart] = (
                hid_ref[:, at : at + j_quart].astype(F32) + fin[j, 4 * q : 4 * q + 4, :]
            ).astype(BF)

    for k in range(1, n_z):
        z_copy(k).wait_send()
    for k in range(n_z):
        for f in range(3):
            xy_copy(f, k, z).wait_send()
        co_copy(k, z).wait_send()
    for f in range(3):
        fw_copy(f).wait_send()
    for j in range(n_j):
        for i in range(n_exp):
            for k in range(1, n_dp):
                ob_copy(i, j, k).wait_send()
        for k in range(1, n_z):
            zz_copy(j, k).wait_send()


def fused(hidden_in, norm_gain, expert_ids, gate_share, w_gate, w_up, w_down):
    n_dp, n_z = lax.axis_size("dp"), lax.axis_size("expert")
    tok, d_model = hidden_in.shape
    slots, units, _ = w_gate.shape
    n_exp = slots // SPLIT
    ff = SPLIT * units
    n_gu = 3
    chunk = ff // n_gu
    n_j = 4
    j_cols = d_model // n_j
    j_quart = j_cols // QUART
    flat = (slots * units, d_model)
    dma = pltpu.SemaphoreType.DMA
    vmem = pl.BlockSpec(memory_space=pltpu.VMEM)
    hbm = pl.BlockSpec(memory_space=pl.ANY)
    wide = d_model // QUART + META
    return pl.pallas_call(
        functools.partial(moe_kernel, n_dp, n_z, n_exp, chunk, n_gu, n_j),
        out_shape=jax.ShapeDtypeStruct((tok, d_model), BF),
        in_specs=[vmem] * 4 + [hbm] * 3,
        out_specs=vmem,
        scratch_shapes=[
            pltpu.VMEM((n_dp * n_z, ROWS, wide), BF),
            pltpu.VMEM((n_exp, n_dp * 4, d_model), BF),
            pltpu.VMEM((PAIRS, chunk, d_model), BF),
            pltpu.VMEM((PAIRS, chunk, d_model), BF),
            pltpu.VMEM((n_j, ff, j_cols), BF),
            pltpu.VMEM((n_gu, n_dp * 4, chunk), BF),
            pltpu.VMEM((ROWS, wide), F32),
            pltpu.VMEM((n_exp, n_j, n_dp, ROWS, j_quart), BF),
            pltpu.VMEM((n_exp, n_j, n_dp, ROWS, j_quart), BF),
            pltpu.VMEM((n_j, n_z, ROWS, j_quart), BF),
            pltpu.VMEM((n_j, n_z, ROWS, j_quart), BF),
            pltpu.VMEM((n_j, n_z, ROWS, j_quart), F32),
            pltpu.VMEM((n_j, ROWS, j_quart), F32),
            pltpu.VMEM((n_exp, n_z * ROWS, n_dp * ROWS), BF),
            dma((PAIRS,)), dma((PAIRS,)), dma((n_j,)),
            dma((n_z - 1,)), dma((n_z - 1,)),
            dma((3, n_z)), dma((3, n_z)),
            dma((n_z,)), dma((n_z,)),
            dma((3,)), dma((3,)),
            dma((n_exp, n_j, n_dp - 1)), dma((n_exp, n_j, n_dp - 1)),
            dma((n_j, n_z - 1)), dma((n_j, n_z - 1)),
        ],
        compiler_params=pltpu.CompilerParams(
            collective_id=0, has_side_effects=True, vmem_limit_bytes=60 * 1024 * 1024
        ),
        cost_estimate=pl.CostEstimate(
            flops=6 * slots * units * d_model * n_dp * 4,
            bytes_accessed=6 * slots * units * d_model,
            transcendentals=slots * units * n_dp * 4,
        ),
        name="routed_experts",
    )(
        hidden_in, norm_gain.reshape(1, d_model), expert_ids, gate_share,
        w_gate.reshape(flat), w_up.reshape(flat), w_down.reshape(flat),
    )


def by_parts(hidden_in, norm_gain, expert_ids, gate_share, w_gate, w_up, w_down):
    dp_count = lax.axis_size("dp")
    col_count = lax.axis_size("expert")
    row_index = lax.axis_index("dp")
    column = lax.axis_index("expert")
    tok_dev = hidden_in.shape[0]
    model_width = hidden_in.shape[1]
    slot_dev = w_gate.shape[0]
    block_units = w_gate.shape[1]
    experts_row = EXPERTS // dp_count
    per_dev = max(1, slot_dev // SPLIT)
    runs_dev = slot_dev // per_dev
    capacity = tok_dev * col_count // 4
    resid = hidden_in.astype(jnp.float32)
    inv_rms = lax.rsqrt(jnp.mean(resid * resid, axis=1, keepdims=True) + 1e-06)
    normed = (resid * inv_rms * norm_gain.astype(jnp.float32)[None, :]).astype(jnp.bfloat16)
    row_x, row_share, row_ids = (
        lax.all_gather(normed, "expert", axis=0, tiled=True),
        lax.all_gather(gate_share, "expert", axis=0, tiled=True),
        lax.all_gather(expert_ids, "expert", axis=0, tiled=True),
    )
    tok_row = row_x.shape[0]
    flat_ids = row_ids.reshape(-1)
    onehot = (flat_ids[:, None] == jnp.arange(EXPERTS, dtype=jnp.int32)[None, :]).astype(jnp.int32)
    order_pos = jnp.sum((jnp.cumsum(onehot, axis=0) - onehot) * onehot, axis=1)
    slot_keys = (flat_ids * capacity + order_pos).reshape(tok_row, row_ids.shape[1])
    dest_rows = jnp.arange(dp_count, dtype=jnp.int32)[:, None]
    held = (dest_rows * col_count + column) * slot_dev // SPLIT + jnp.arange(
        per_dev, dtype=jnp.int32
    )[None, :]
    targets = held[:, :, None] * capacity + jnp.arange(capacity, dtype=jnp.int32)[None, None, :]
    matches = slot_keys[None, None, None, :, :] == targets[:, :, :, None, None]
    share_f = row_share.astype(jnp.float32)[None, None, None, :, :]
    weighted = jnp.sum(jnp.where(matches, share_f, 0.0), axis=4).astype(jnp.bfloat16)
    gate_w = w_gate.reshape(per_dev, runs_dev, block_units, model_width)
    up_w = w_up.reshape(per_dev, runs_dev, block_units, model_width)
    down_w = w_down.reshape(per_dev, runs_dev, block_units, model_width)
    part_rows = capacity // col_count
    row_experts = dest_rows * experts_row + jnp.arange(experts_row, dtype=jnp.int32)[None, :]
    section_targets = (
        row_experts[:, :, None] * capacity
        + column * part_rows
        + jnp.arange(part_rows, dtype=jnp.int32)[None, None, :]
    )
    section_hits = jnp.any(
        slot_keys[None, None, None, :, :] == section_targets[:, :, :, None, None], axis=4
    )
    section_blocks = jnp.einsum(
        "qmst,td->qmsd",
        section_hits.astype(jnp.bfloat16),
        row_x,
        preferred_element_type=jnp.float32,
    ).astype(jnp.bfloat16)
    landed = lax.all_to_all(section_blocks, "dp", split_axis=0, concat_axis=0, tiled=True)
    own_first = (row_index * col_count + column) * slot_dev // SPLIT - row_index * experts_row
    own_rows = lax.dynamic_slice_in_dim(
        lax.all_gather(landed, "expert", axis=2, tiled=True), own_first, per_dev, 1
    )
    gate_vals = jnp.einsum("qisd,igfd->qisgf", own_rows, gate_w, preferred_element_type=jnp.float32)
    up_vals = jnp.einsum("qisd,igfd->qisgf", own_rows, up_w, preferred_element_type=jnp.float32)
    activated = (jax.nn.silu(gate_vals) * up_vals).astype(jnp.bfloat16)
    projected = jnp.einsum(
        "qisgf,igfd->qisd", activated, down_w, preferred_element_type=jnp.float32
    )
    partial_value = projected.astype(jnp.bfloat16)
    returned = lax.all_to_all(partial_value, "dp", split_axis=0, concat_axis=0, tiled=True)
    routed = lax.psum_scatter(
        jnp.einsum("qist,qisd->td", weighted, returned, preferred_element_type=jnp.float32).astype(
            jnp.bfloat16
        ),
        "expert",
        scatter_dimension=0,
        tiled=True,
    ).astype(jnp.float32)
    return (resid + routed).astype(jnp.bfloat16)


def body(hidden_in, norm_gain, expert_ids, gate_share, w_gate, w_up, w_down):
    args = (hidden_in, norm_gain, expert_ids, gate_share, w_gate, w_up, w_down)
    whole_experts = w_gate.shape[0] % SPLIT == 0
    if whole_experts and lax.axis_size("dp") == 8 and lax.axis_size("expert") == 4:
        return fused(*args)
    return by_parts(*args)


def solution(mesh):
    placed = (
        P(("dp", "expert"), None),
        P(),
        P(("dp", "expert"), None),
        P(("dp", "expert"), None),
        P(("dp", "expert"), None, None),
        P(("dp", "expert"), None, None),
        P(("dp", "expert"), None, None),
    )
    return jax.shard_map(
        body, mesh=mesh, in_specs=placed, out_specs=P(("dp", "expert"), None), check_vma=False
    )
```

```python
import functools

import jax
import jax.numpy as jnp
from jax import lax
from jax.experimental import pallas as pl
from jax.experimental.pallas import tpu as pltpu
from jax.sharding import PartitionSpec as P

EXPERTS = 64
SPLIT = 8

ROWS = 16
QUART = 4
META = 128
PAIRS = 5
MESH = pl.DeviceIdType.MESH
BF = jnp.bfloat16
F32 = jnp.float32


def iota(shape, dim):
    return lax.broadcasted_iota(jnp.int32, shape, dim)


def dot(a, b):
    return jnp.dot(a, b, preferred_element_type=F32)


def dot_nt(a, b):
    return lax.dot_general(a, b, (((1,), (1,)), ((), ())), preferred_element_type=F32)


def tok_of(r):
    return (r // ROWS) % QUART * 4 + r % 4


def quarter_of(r):
    return r % ROWS // 4


def moe_kernel(
    n_dp, n_z, n_exp, chunk, n_gu, n_j,
    hid_ref, gain_ref, ids_ref, share_ref, wg, wu, wd,
    out_ref,
    buf, xs, gbuf, ubuf, dbuf, act, pay, ob_send, ob_recv, z_send, z_recv, z_own, fin, wmat,
    g_sem, u_sem, d_sem,
    zs_s, zs_r, xy_s, xy_r, co_s, co_r, fw_s, fw_r, ob_s, ob_r, zz_s, zz_r,
):
    dp = lax.axis_index("dp")
    z = lax.axis_index("expert")
    d_model = hid_ref.shape[1]
    ff = n_gu * chunk
    quarter = d_model // QUART
    j_cols = d_model // n_j
    j_quart = j_cols // QUART
    cap_rows = n_dp * 4
    n_rows = n_dp * n_z * ROWS

    def gu_copies(p):
        slot = lax.rem(p, PAIRS)
        rows = pl.ds(pl.multiple_of(p * chunk, chunk), chunk)
        return (
            pltpu.make_async_copy(wg.at[rows], gbuf.at[slot], g_sem.at[slot]),
            pltpu.make_async_copy(wu.at[rows], ubuf.at[slot], u_sem.at[slot]),
        )

    def d_copy(i, j):
        return pltpu.make_async_copy(
            wd.at[
                pl.ds(pl.multiple_of(i * ff, ff), ff),
                pl.ds(pl.multiple_of(j * j_cols, j_cols), j_cols),
            ],
            dbuf.at[j],
            d_sem.at[j],
        )

    def start_gu(p):
        a, b = gu_copies(p)
        a.start()
        b.start()

    n_pairs = n_exp * n_gu
    first_copies = []
    for p in range(n_gu):
        first_copies.extend(gu_copies(jnp.int32(p)))
    first_copies.extend(d_copy(jnp.int32(0), jnp.int32(j)) for j in range(n_j))
    for p in range(n_gu, min(PAIRS, n_pairs)):
        first_copies.extend(gu_copies(jnp.int32(p)))
    first_copies = iter(first_copies)

    def stream(count):
        for _, copy in zip(range(count), first_copies):
            copy.start()

    stream(2)

    core = lax.rem(dp, 2)
    xc = lax.rem(lax.div(dp, 2), 2)
    yc = lax.div(dp, 4)
    flip_c = 1 - 2 * core
    flip_x = 2 - 4 * xc
    flip_y = 4 - 8 * yc
    sib = dp + flip_c
    flips = (flip_x, flip_y, flip_x + flip_y)
    barrier = pltpu.get_barrier_semaphore()
    for k in range(1, n_dp):
        pl.semaphore_signal(
            barrier, inc=1, device_id=(lax.rem(dp + k, n_dp), z), device_id_type=MESH
        )
    for k in range(1, n_z):
        pl.semaphore_signal(
            barrier, inc=1, device_id=(dp, lax.rem(z + k, n_z)), device_id_type=MESH
        )

    resid = hid_ref[...].astype(F32)
    inv_rms = lax.rsqrt(jnp.mean(resid * resid, axis=1, keepdims=True) + 1e-06)
    normed = resid * inv_rms * gain_ref[...].astype(F32).reshape(1, d_model)
    put = iota((8, META), 1) - iota((8, META), 0)
    meta = dot(ids_ref[...].astype(F32).astype(BF), (put == 0).astype(F32).astype(BF)) + dot(
        share_ref[...], (put == 8).astype(F32).astype(BF)
    )
    for j in range(QUART):
        pay[4 * j : 4 * j + 4, 0:quarter] = normed[:, j * quarter : (j + 1) * quarter]
        pay[4 * j : 4 * j + 4, quarter : quarter + META] = meta
    me = dp * n_z + z
    buf[me] = pay[...].astype(BF)

    pl.semaphore_wait(barrier, n_dp - 1 + n_z - 1)

    def remote(src, dst, s, r, to):
        return pltpu.make_async_remote_copy(
            src_ref=src, dst_ref=dst, send_sem=s, recv_sem=r, device_id=to, device_id_type=MESH
        )

    def z_copy(k):
        blk = buf.at[me]
        return remote(blk, blk, zs_s.at[k - 1], zs_r.at[k - 1], (dp, lax.rem(z + k, n_z)))

    def xy_copy(f, k, zb):
        blk = buf.at[dp * n_z + zb]
        return remote(blk, blk, xy_s.at[f, k], xy_r.at[f, k], (dp + flips[f], z))

    def co_copy(k, zb):
        blk = buf.at[dp * n_z + zb]
        return remote(blk, blk, co_s.at[k], co_r.at[k], (sib, z))

    def fw_copy(f):
        blk = buf.at[pl.ds((dp + flips[f]) * n_z, n_z)]
        return remote(blk, blk, fw_s.at[f], fw_r.at[f], (sib, z))

    for k in range(1, n_z):
        z_copy(k).start()
    for k in range(n_z):
        if k > 0:
            stream(1)
        zb = lax.rem(z + n_z - k, n_z)
        if k > 0:
            z_copy(k).wait_recv()
        for f in range(3):
            xy_copy(f, k, zb).start()
        co_copy(k, zb).start()

    tr, tc = iota((n_rows, 1), 0), iota((1, n_rows), 1)
    before = (
        (tr // (n_z * ROWS) == tc // (n_z * ROWS))
        & (quarter_of(tr) == 0)
        & (tok_of(tr) < tok_of(tc))
    )
    before = before.astype(F32).astype(BF)
    stream(2)

    grp = n_z * ROWS
    meta_g = buf[pl.ds(dp * n_z, n_z), :, quarter : quarter + META].reshape(grp, META).astype(F32)
    gr, gc = iota((grp, 1), 0), iota((1, grp), 1)
    before_g = ((quarter_of(gc) == 0) & (tok_of(gc) < tok_of(gr))).astype(F32).astype(BF)
    lanes = n_dp * ROWS
    lc = iota((1, lanes), 1)
    lane_first = ((lc // ROWS * n_z + z) * n_exp).astype(F32)
    same_q = quarter_of(gr) == quarter_of(lc)
    lane_slot = (lc % 4).astype(F32)
    for i in range(n_exp):
        hits = jnp.zeros((grp, lanes), F32)
        shares = jnp.zeros((grp, lanes), F32)
        for k in range(8):
            match = meta_g[:, k : k + 1] == lane_first + i
            hits = hits + match.astype(F32)
            shares = shares + jnp.where(match, meta_g[:, 8 + k : 9 + k], 0.0)
        rank = dot(before_g, hits.astype(BF))
        keep = (hits > 0) & (rank == lane_slot) & same_q
        wmat[i] = jnp.where(keep, shares, 0.0).astype(BF)

    for f in range(3):
        for k in range(n_z):
            xy_copy(f, k, z).wait_recv()
        fw_copy(f).start()
        stream(2)
    for k in range(n_z):
        co_copy(k, z).wait_recv()
    for f in range(3):
        fw_copy(f).wait_recv()
    stream(n_pairs * 2 + n_j)

    meta_all = buf[:, :, quarter : quarter + META].reshape(n_rows, META)
    pick = (iota((16, META), 0) == iota((16, META), 1)).astype(F32).astype(BF)
    meta_t = dot_nt(pick, meta_all)
    ids_t = meta_t[0:8]
    first = (me * n_exp).astype(F32)
    lane_q = quarter_of(tc)
    group = (tc // (n_z * ROWS) * 4).astype(F32)
    slot_iota = iota((n_exp * cap_rows, 1), 0)
    key = jnp.full((1, n_rows), -1.0, F32)
    for i in range(n_exp):
        hit = jnp.sum((ids_t == first + i).astype(F32), axis=0, keepdims=True)
        rank = dot(jnp.broadcast_to(hit, (8, n_rows)).astype(BF), before)[0:1]
        own_key = jnp.where(hit > 0, group + rank + i * cap_rows, -1.0)
        key = jnp.where(slot_iota // cap_rows == i, own_key, key)
    slot_f = slot_iota.astype(F32)
    for j in range(QUART):
        sel = ((slot_f == key) & (lane_q == j)).astype(F32).astype(BF)
        xs[:, :, j * quarter : (j + 1) * quarter] = (
            dot(sel, buf[:, :, 0:quarter].reshape(n_rows, quarter))
            .astype(BF)
            .reshape(n_exp, cap_rows, quarter)
        )

    def ob_copy(i, j, k):
        to = lax.rem(dp + k, n_dp)
        return remote(
            ob_send.at[i, j, to], ob_recv.at[i, j, dp], ob_s.at[i, j, k - 1],
            ob_r.at[i, j, k - 1], (to, z),
        )

    pr, pc = iota((lanes, 1), 0), iota((1, cap_rows), 1)
    same_slot = pr // ROWS * 4 + pr % 4 == pc
    spread = [
        (same_slot & (quarter_of(pr) == q)).astype(F32).astype(BF) for q in range(QUART)
    ]

    def expert(i, carry):
        def gu_step(c, carry):
            p = i * n_gu + c
            slot = lax.rem(p, PAIRS)
            a, b = gu_copies(p)
            a.wait()
            gate = dot_nt(xs[i], gbuf[slot])
            b.wait()
            up = dot_nt(xs[i], ubuf[slot])
            act[c] = (gate / (1.0 + jnp.exp(-gate)) * up).astype(BF)

            @pl.when(p + PAIRS < n_pairs)
            def _():
                start_gu(p + PAIRS)

            return carry

        lax.fori_loop(0, n_gu, gu_step, 0)

        def d_step(j, carry):
            d_copy(i, j).wait()
            total = dot(act[0], dbuf[j, 0:chunk, :])
            for c in range(1, n_gu):
                total = total + dot(act[c], dbuf[j, c * chunk : (c + 1) * chunk, :])
            total = total.astype(BF)

            @pl.when(i + 1 < n_exp)
            def _():
                d_copy(i + 1, j).start()

            rows = dot(spread[0], total[:, 0:j_quart])
            for q in range(1, QUART):
                rows = rows + dot(spread[q], total[:, q * j_quart : (q + 1) * j_quart])
            ob_send[i, j] = rows.astype(BF).reshape(n_dp, ROWS, j_quart)
            for k in range(1, n_dp):
                ob_copy(i, j, k).start()
            ob_recv[i, j, dp] = ob_send[i, j, dp]
            return carry

        lax.fori_loop(0, n_j, d_step, 0)
        return carry

    lax.fori_loop(0, n_exp, expert, 0)

    def zz_copy(j, k):
        to = lax.rem(z + k, n_z)
        return remote(
            z_send.at[j, to], z_recv.at[j, z], zz_s.at[j, k - 1], zz_r.at[j, k - 1], (dp, to)
        )

    for j in range(n_j):
        part = jnp.zeros((grp, j_quart), F32)
        for i in range(n_exp):
            for k in range(1, n_dp):
                ob_copy(i, j, k).wait_recv()
            part = part + dot(wmat[i], ob_recv[i, j].reshape(lanes, j_quart))
        z_send[j] = part.astype(BF).reshape(n_z, ROWS, j_quart)
        z_own[j] = part.reshape(n_z, ROWS, j_quart)
        for k in range(1, n_z):
            zz_copy(j, k).start()
    for j in range(n_j):
        total = z_own[j, z]
        for k in range(1, n_z):
            zz_copy(j, k).wait_recv()
            total = total + z_recv[j, lax.rem(z + n_z - k, n_z)].astype(F32)
        fin[j] = total
        for q in range(QUART):
            at = j * j_cols + q * j_quart
            out_ref[:, at : at + j_quart] = (
                hid_ref[:, at : at + j_quart].astype(F32) + fin[j, 4 * q : 4 * q + 4, :]
            ).astype(BF)

    for k in range(1, n_z):
        z_copy(k).wait_send()
    for k in range(n_z):
        for f in range(3):
            xy_copy(f, k, z).wait_send()
        co_copy(k, z).wait_send()
    for f in range(3):
        fw_copy(f).wait_send()
    for j in range(n_j):
        for i in range(n_exp):
            for k in range(1, n_dp):
                ob_copy(i, j, k).wait_send()
        for k in range(1, n_z):
            zz_copy(j, k).wait_send()


def fused(hidden_in, norm_gain, expert_ids, gate_share, w_gate, w_up, w_down):
    n_dp, n_z = lax.axis_size("dp"), lax.axis_size("expert")
    tok, d_model = hidden_in.shape
    slots, units, _ = w_gate.shape
    n_exp = slots // SPLIT
    ff = SPLIT * units
    n_gu = 3
    chunk = ff // n_gu
    n_j = 4
    j_cols = d_model // n_j
    j_quart = j_cols // QUART
    flat = (slots * units, d_model)
    dma = pltpu.SemaphoreType.DMA
    vmem = pl.BlockSpec(memory_space=pltpu.VMEM)
    hbm = pl.BlockSpec(memory_space=pl.ANY)
    wide = d_model // QUART + META
    return pl.pallas_call(
        functools.partial(moe_kernel, n_dp, n_z, n_exp, chunk, n_gu, n_j),
        out_shape=jax.ShapeDtypeStruct((tok, d_model), BF),
        in_specs=[vmem] * 4 + [hbm] * 3,
        out_specs=vmem,
        scratch_shapes=[
            pltpu.VMEM((n_dp * n_z, ROWS, wide), BF),
            pltpu.VMEM((n_exp, n_dp * 4, d_model), BF),
            pltpu.VMEM((PAIRS, chunk, d_model), BF),
            pltpu.VMEM((PAIRS, chunk, d_model), BF),
            pltpu.VMEM((n_j, ff, j_cols), BF),
            pltpu.VMEM((n_gu, n_dp * 4, chunk), BF),
            pltpu.VMEM((ROWS, wide), F32),
            pltpu.VMEM((n_exp, n_j, n_dp, ROWS, j_quart), BF),
            pltpu.VMEM((n_exp, n_j, n_dp, ROWS, j_quart), BF),
            pltpu.VMEM((n_j, n_z, ROWS, j_quart), BF),
            pltpu.VMEM((n_j, n_z, ROWS, j_quart), BF),
            pltpu.VMEM((n_j, n_z, ROWS, j_quart), F32),
            pltpu.VMEM((n_j, ROWS, j_quart), F32),
            pltpu.VMEM((n_exp, n_z * ROWS, n_dp * ROWS), BF),
            dma((PAIRS,)), dma((PAIRS,)), dma((n_j,)),
            dma((n_z - 1,)), dma((n_z - 1,)),
            dma((3, n_z)), dma((3, n_z)),
            dma((n_z,)), dma((n_z,)),
            dma((3,)), dma((3,)),
            dma((n_exp, n_j, n_dp - 1)), dma((n_exp, n_j, n_dp - 1)),
            dma((n_j, n_z - 1)), dma((n_j, n_z - 1)),
        ],
        compiler_params=pltpu.CompilerParams(
            collective_id=0, has_side_effects=True, vmem_limit_bytes=60 * 1024 * 1024
        ),
        cost_estimate=pl.CostEstimate(
            flops=6 * slots * units * d_model * n_dp * 4,
            bytes_accessed=6 * slots * units * d_model,
            transcendentals=slots * units * n_dp * 4,
        ),
        name="routed_experts",
    )(
        hidden_in, norm_gain, expert_ids, gate_share,
        w_gate.reshape(flat), w_up.reshape(flat), w_down.reshape(flat),
    )


def by_parts(hidden_in, norm_gain, expert_ids, gate_share, w_gate, w_up, w_down):
    dp_count = lax.axis_size("dp")
    col_count = lax.axis_size("expert")
    row_index = lax.axis_index("dp")
    column = lax.axis_index("expert")
    tok_dev = hidden_in.shape[0]
    model_width = hidden_in.shape[1]
    slot_dev = w_gate.shape[0]
    block_units = w_gate.shape[1]
    experts_row = EXPERTS // dp_count
    per_dev = max(1, slot_dev // SPLIT)
    runs_dev = slot_dev // per_dev
    capacity = tok_dev * col_count // 4
    resid = hidden_in.astype(jnp.float32)
    inv_rms = lax.rsqrt(jnp.mean(resid * resid, axis=1, keepdims=True) + 1e-06)
    normed = (resid * inv_rms * norm_gain.astype(jnp.float32)[None, :]).astype(jnp.bfloat16)
    row_x, row_share, row_ids = (
        lax.all_gather(normed, "expert", axis=0, tiled=True),
        lax.all_gather(gate_share, "expert", axis=0, tiled=True),
        lax.all_gather(expert_ids, "expert", axis=0, tiled=True),
    )
    tok_row = row_x.shape[0]
    flat_ids = row_ids.reshape(-1)
    onehot = (flat_ids[:, None] == jnp.arange(EXPERTS, dtype=jnp.int32)[None, :]).astype(jnp.int32)
    order_pos = jnp.sum((jnp.cumsum(onehot, axis=0) - onehot) * onehot, axis=1)
    slot_keys = (flat_ids * capacity + order_pos).reshape(tok_row, row_ids.shape[1])
    dest_rows = jnp.arange(dp_count, dtype=jnp.int32)[:, None]
    held = (dest_rows * col_count + column) * slot_dev // SPLIT + jnp.arange(
        per_dev, dtype=jnp.int32
    )[None, :]
    targets = held[:, :, None] * capacity + jnp.arange(capacity, dtype=jnp.int32)[None, None, :]
    matches = slot_keys[None, None, None, :, :] == targets[:, :, :, None, None]
    share_f = row_share.astype(jnp.float32)[None, None, None, :, :]
    weighted = jnp.sum(jnp.where(matches, share_f, 0.0), axis=4).astype(jnp.bfloat16)
    gate_w = w_gate.reshape(per_dev, runs_dev, block_units, model_width)
    up_w = w_up.reshape(per_dev, runs_dev, block_units, model_width)
    down_w = w_down.reshape(per_dev, runs_dev, block_units, model_width)
    part_rows = capacity // col_count
    row_experts = dest_rows * experts_row + jnp.arange(experts_row, dtype=jnp.int32)[None, :]
    section_targets = (
        row_experts[:, :, None] * capacity
        + column * part_rows
        + jnp.arange(part_rows, dtype=jnp.int32)[None, None, :]
    )
    section_hits = jnp.any(
        slot_keys[None, None, None, :, :] == section_targets[:, :, :, None, None], axis=4
    )
    section_blocks = jnp.einsum(
        "qmst,td->qmsd",
        section_hits.astype(jnp.bfloat16),
        row_x,
        preferred_element_type=jnp.float32,
    ).astype(jnp.bfloat16)
    landed = lax.all_to_all(section_blocks, "dp", split_axis=0, concat_axis=0, tiled=True)
    own_first = (row_index * col_count + column) * slot_dev // SPLIT - row_index * experts_row
    own_rows = lax.dynamic_slice_in_dim(
        lax.all_gather(landed, "expert", axis=2, tiled=True), own_first, per_dev, 1
    )
    gate_vals = jnp.einsum("qisd,igfd->qisgf", own_rows, gate_w, preferred_element_type=jnp.float32)
    up_vals = jnp.einsum("qisd,igfd->qisgf", own_rows, up_w, preferred_element_type=jnp.float32)
    activated = (jax.nn.silu(gate_vals) * up_vals).astype(jnp.bfloat16)
    projected = jnp.einsum(
        "qisgf,igfd->qisd", activated, down_w, preferred_element_type=jnp.float32
    )
    partial_value = projected.astype(jnp.bfloat16)
    returned = lax.all_to_all(partial_value, "dp", split_axis=0, concat_axis=0, tiled=True)
    routed = lax.psum_scatter(
        jnp.einsum("qist,qisd->td", weighted, returned, preferred_element_type=jnp.float32).astype(
            jnp.bfloat16
        ),
        "expert",
        scatter_dimension=0,
        tiled=True,
    ).astype(jnp.float32)
    return (resid + routed).astype(jnp.bfloat16)


def body(hidden_in, norm_gain, expert_ids, gate_share, w_gate, w_up, w_down):
    args = (hidden_in, norm_gain, expert_ids, gate_share, w_gate, w_up, w_down)
    whole_experts = w_gate.shape[0] % SPLIT == 0
    if whole_experts and lax.axis_size("dp") == 8 and lax.axis_size("expert") == 4:
        return fused(*args)
    return by_parts(*args)


def solution(mesh):
    placed = (
        P(("dp", "expert"), None),
        P(),
        P(("dp", "expert"), None),
        P(("dp", "expert"), None),
        P(("dp", "expert"), None, None),
        P(("dp", "expert"), None, None),
        P(("dp", "expert"), None, None),
    )
    return jax.shard_map(
        body, mesh=mesh, in_specs=placed, out_specs=P(("dp", "expert"), None), check_vma=False
    )
```

```python
import functools

import jax
import jax.numpy as jnp
from jax import lax
from jax.experimental import pallas as pl
from jax.experimental.pallas import tpu as pltpu
from jax.sharding import PartitionSpec as P

EXPERTS = 64
SPLIT = 8

ROWS = 16
QUART = 4
META = 128
WEIGHT_SLOTS = 9
HALVES = 2
MESH = pl.DeviceIdType.MESH
BF = jnp.bfloat16
F32 = jnp.float32


def iota(shape, dim):
    return lax.broadcasted_iota(jnp.int32, shape, dim)


def dot(a, b):
    return jnp.dot(a, b, preferred_element_type=F32)


def dot_nt(a, b):
    return lax.dot_general(a, b, (((1,), (1,)), ((), ())), preferred_element_type=F32)


def tok_of(r):
    return (r // ROWS) % QUART * 4 + r % 4


def quarter_of(r):
    return r % ROWS // 4


def moe_kernel(
    n_dp, n_z, n_exp, ff, n_j,
    hid_ref, gain_ref, ids_ref, share_ref, wg, wu, wd,
    out_ref,
    buf, meta_buf, xs, wbuf, acc_g, acc_u, act, pay, ob_send, ob_recv, z_send, z_recv, z_own,
    fin, wmat,
    w_sem,
    zs_s, zs_r, xy_s, xy_r, co_s, co_r, fw_s, fw_r,
    mz_s, mz_r, mxy_s, mxy_r, mco_s, mco_r, mfw_s, mfw_r,
    ob_s, ob_r, zz_s, zz_r,
):
    dp = lax.axis_index("dp")
    z = lax.axis_index("expert")
    d_model = hid_ref.shape[1]
    half = d_model // HALVES
    quarter = half // QUART
    j_cols = d_model // n_j
    j_quart = j_cols // QUART
    cap_rows = n_dp * 4
    n_rows = n_dp * n_z * ROWS

    n_head = 2 * n_exp

    def w_copy(ref, i, h, n):
        slot = lax.rem(n, WEIGHT_SLOTS)
        return pltpu.make_async_copy(
            ref.at[
                pl.ds(pl.multiple_of(i * ff, ff), ff),
                pl.ds(pl.multiple_of(h * half, half), half),
            ],
            wbuf.at[slot],
            w_sem.at[slot],
        )

    def chunk(n):
        if n < n_head:
            return w_copy((wg, wu)[n % 2], jnp.int32(n // 2), 0, jnp.int32(n))
        i, at = divmod(n - n_head, 4)
        ref, h = ((wg, 1), (wu, 1), (wd, 0), (wd, 1))[at]
        return w_copy(ref, jnp.int32(i), h, jnp.int32(n))

    n_chunks = n_head + 4 * n_exp
    first_copies = iter([chunk(n) for n in range(min(WEIGHT_SLOTS, n_chunks))])

    def stream(count):
        for _, copy in zip(range(count), first_copies):
            copy.start()

    stream(2)

    core = lax.rem(dp, 2)
    xc = lax.rem(lax.div(dp, 2), 2)
    yc = lax.div(dp, 4)
    flip_c = 1 - 2 * core
    flip_x = 2 - 4 * xc
    flip_y = 4 - 8 * yc
    sib = dp + flip_c
    flips = (flip_x, flip_y, flip_x + flip_y)
    barrier = pltpu.get_barrier_semaphore()
    for k in range(1, n_dp):
        pl.semaphore_signal(
            barrier, inc=1, device_id=(lax.rem(dp + k, n_dp), z), device_id_type=MESH
        )
    for k in range(1, n_z):
        pl.semaphore_signal(
            barrier, inc=1, device_id=(dp, lax.rem(z + k, n_z)), device_id_type=MESH
        )

    resid = hid_ref[...].astype(F32)
    inv_rms = lax.rsqrt(jnp.mean(resid * resid, axis=1, keepdims=True) + 1e-06)
    normed = resid * inv_rms * gain_ref[...].astype(F32).reshape(1, d_model)
    put = iota((8, META), 1) - iota((8, META), 0)
    meta = dot(ids_ref[...].astype(F32).astype(BF), (put == 0).astype(F32).astype(BF)) + dot(
        share_ref[...], (put == 8).astype(F32).astype(BF)
    )
    me = dp * n_z + z
    for h in range(HALVES):
        for q in range(QUART):
            at = h * half + q * quarter
            pay[h, 4 * q : 4 * q + 4, 0:quarter] = normed[:, at : at + quarter]
            if h == 0:
                pay[0, 4 * q : 4 * q + 4, quarter : quarter + META] = meta
    meta_buf[me] = pay[0].astype(BF)
    buf[me] = pay[1, :, 0:quarter].astype(BF)

    pl.semaphore_wait(barrier, n_dp - 1 + n_z - 1)

    def remote(src, dst, s, r, to):
        return pltpu.make_async_remote_copy(
            src_ref=src, dst_ref=dst, send_sem=s, recv_sem=r, device_id=to, device_id_type=MESH
        )

    held = (meta_buf, buf)
    sems = (
        (mz_s, mz_r, mxy_s, mxy_r, mco_s, mco_r, mfw_s, mfw_r),
        (zs_s, zs_r, xy_s, xy_r, co_s, co_r, fw_s, fw_r),
    )

    def z_copy(h, k):
        blk = held[h].at[me]
        s, r = sems[h][0:2]
        return remote(blk, blk, s.at[k - 1], r.at[k - 1], (dp, lax.rem(z + k, n_z)))

    def xy_copy(h, f, k, zb):
        blk = held[h].at[dp * n_z + zb]
        s, r = sems[h][2:4]
        return remote(blk, blk, s.at[f, k], r.at[f, k], (dp + flips[f], z))

    def co_copy(h, k, zb):
        blk = held[h].at[dp * n_z + zb]
        s, r = sems[h][4:6]
        return remote(blk, blk, s.at[k], r.at[k], (sib, z))

    def fw_copy(h, f):
        blk = held[h].at[pl.ds((dp + flips[f]) * n_z, n_z)]
        s, r = sems[h][6:8]
        return remote(blk, blk, s.at[f], r.at[f], (sib, z))

    def forward(h):
        for f in range(3):
            for k in range(n_z):
                xy_copy(h, f, k, z).wait_recv()
            fw_copy(h, f).start()

    def arrived(h):
        for k in range(n_z):
            co_copy(h, k, z).wait_recv()
        for f in range(3):
            fw_copy(h, f).wait_recv()

    for h in range(HALVES):
        for k in range(1, n_z):
            z_copy(h, k).start()
    for h in range(HALVES):
        for k in range(n_z):
            zb = lax.rem(z + n_z - k, n_z)
            if k > 0:
                z_copy(h, k).wait_recv()
            for f in range(3):
                xy_copy(h, f, k, zb).start()
            co_copy(h, k, zb).start()
        stream(2)

    tr, tc = iota((n_rows, 1), 0), iota((1, n_rows), 1)
    before = (
        (tr // (n_z * ROWS) == tc // (n_z * ROWS))
        & (quarter_of(tr) == 0)
        & (tok_of(tr) < tok_of(tc))
    )
    before = before.astype(F32).astype(BF)

    forward(0)
    stream(WEIGHT_SLOTS)

    grp = n_z * ROWS
    meta_g = (
        meta_buf[pl.ds(dp * n_z, n_z), :, quarter : quarter + META].reshape(grp, META).astype(F32)
    )
    gr, gc = iota((grp, 1), 0), iota((1, grp), 1)
    before_g = ((quarter_of(gc) == 0) & (tok_of(gc) < tok_of(gr))).astype(F32).astype(BF)
    lanes = n_dp * ROWS
    lc = iota((1, lanes), 1)
    lane_first = ((lc // ROWS * n_z + z) * n_exp).astype(F32)
    same_q = quarter_of(gr) == quarter_of(lc)
    lane_slot = (lc % 4).astype(F32)
    for i in range(n_exp):
        hits = jnp.zeros((grp, lanes), F32)
        shares = jnp.zeros((grp, lanes), F32)
        for k in range(8):
            match = meta_g[:, k : k + 1] == lane_first + i
            hits = hits + match.astype(F32)
            shares = shares + jnp.where(match, meta_g[:, 8 + k : 9 + k], 0.0)
        rank = dot(before_g, hits.astype(BF))
        keep = (hits > 0) & (rank == lane_slot) & same_q
        wmat[i] = jnp.where(keep, shares, 0.0).astype(BF)

    arrived(0)

    meta_all = meta_buf[:, :, quarter : quarter + META].reshape(n_rows, META)
    pick = (iota((16, META), 0) == iota((16, META), 1)).astype(F32).astype(BF)
    meta_t = dot_nt(pick, meta_all)
    ids_t = meta_t[0:8]
    first = (me * n_exp).astype(F32)
    lane_q = quarter_of(tc)
    group = (tc // (n_z * ROWS) * 4).astype(F32)
    slot_iota = iota((n_exp * cap_rows, 1), 0)
    key = jnp.full((1, n_rows), -1.0, F32)
    for i in range(n_exp):
        hit = jnp.sum((ids_t == first + i).astype(F32), axis=0, keepdims=True)
        rank = dot(jnp.broadcast_to(hit, (8, n_rows)).astype(BF), before)[0:1]
        own_key = jnp.where(hit > 0, group + rank + i * cap_rows, -1.0)
        key = jnp.where(slot_iota // cap_rows == i, own_key, key)
    chosen = slot_iota.astype(F32) == key

    def pick_rows(h):
        for q in range(QUART):
            sel = (chosen & (lane_q == q)).astype(F32).astype(BF)
            rows = dot(sel, held[h][:, :, 0:quarter].reshape(n_rows, quarter)).astype(BF)
            xs[h, :, :, q * quarter : (q + 1) * quarter] = rows.reshape(n_exp, cap_rows, quarter)

    pick_rows(0)

    def ob_copy(i, j, k):
        to = lax.rem(dp + k, n_dp)
        return remote(
            ob_send.at[i, j, to], ob_recv.at[i, j, dp], ob_s.at[i, j, k - 1],
            ob_r.at[i, j, k - 1], (to, z),
        )

    pr, pc = iota((lanes, 1), 0), iota((1, cap_rows), 1)
    same_slot = pr // ROWS * 4 + pr % 4 == pc
    spread = [
        (same_slot & (quarter_of(pr) == q)).astype(F32).astype(BF) for q in range(QUART)
    ]

    def head(i, carry):
        w_copy(wg, i, 0, 2 * i).wait()
        acc_g[i] = dot_nt(xs[0, i], wbuf[2 * i])
        w_copy(wu, i, 0, 2 * i + 1).wait()
        acc_u[i] = dot_nt(xs[0, i], wbuf[2 * i + 1])

        @pl.when(i == 0)
        def _():
            chunk(WEIGHT_SLOTS).start()
            chunk(WEIGHT_SLOTS + 1).start()
            forward(1)

        return carry

    lax.fori_loop(0, n_exp, head, 0)
    chunk(WEIGHT_SLOTS + 2).start()
    arrived(1)
    pick_rows(1)

    def expert(i, carry):
        n = n_head + 4 * i
        w_copy(wg, i, 1, n).wait()
        gate = acc_g[i] + dot_nt(xs[1, i], wbuf[lax.rem(n, WEIGHT_SLOTS)])
        gate = gate / (1.0 + jnp.exp(-gate))
        w_copy(wu, i, 1, n + 1).wait()
        up = acc_u[i] + dot_nt(xs[1, i], wbuf[lax.rem(n + 1, WEIGHT_SLOTS)])
        act[...] = (gate * up).astype(BF)

        def d_step(j, carry):
            h = j // (n_j // HALVES)
            slot = lax.rem(n + 2 + h, WEIGHT_SLOTS)
            col = pl.multiple_of((j - h * (n_j // HALVES)) * j_cols, j_cols)

            @pl.when(col == 0)
            def _():
                w_copy(wd, i, h, n + 2 + h).wait()

            total = dot(act[...], wbuf[slot, :, pl.ds(col, j_cols)]).astype(BF)
            rows = dot(spread[0], total[:, 0:j_quart])
            for q in range(1, QUART):
                rows = rows + dot(spread[q], total[:, q * j_quart : (q + 1) * j_quart])
            ob_send[i, j] = rows.astype(BF).reshape(n_dp, ROWS, j_quart)
            for k in range(1, n_dp):
                ob_copy(i, j, k).start()
            ob_recv[i, j, dp] = ob_send[i, j, dp]
            return carry

        lax.fori_loop(0, n_j, d_step, 0)
        return carry

    lax.fori_loop(0, n_exp, expert, 0)

    def zz_copy(j, k):
        to = lax.rem(z + k, n_z)
        return remote(
            z_send.at[j, to], z_recv.at[j, z], zz_s.at[j, k - 1], zz_r.at[j, k - 1], (dp, to)
        )

    for j in range(n_j):
        part = jnp.zeros((grp, j_quart), F32)
        for i in range(n_exp):
            for k in range(1, n_dp):
                ob_copy(i, j, k).wait_recv()
            part = part + dot(wmat[i], ob_recv[i, j].reshape(lanes, j_quart))
        z_send[j] = part.astype(BF).reshape(n_z, ROWS, j_quart)
        z_own[j] = part.reshape(n_z, ROWS, j_quart)
        for k in range(1, n_z):
            zz_copy(j, k).start()
    for j in range(n_j):
        total = z_own[j, z]
        for k in range(1, n_z):
            zz_copy(j, k).wait_recv()
            total = total + z_recv[j, lax.rem(z + n_z - k, n_z)].astype(F32)
        fin[j] = total
        for q in range(QUART):
            at = j * j_cols + q * j_quart
            out_ref[:, at : at + j_quart] = (
                hid_ref[:, at : at + j_quart].astype(F32) + fin[j, 4 * q : 4 * q + 4, :]
            ).astype(BF)

    for h in range(HALVES):
        for k in range(1, n_z):
            z_copy(h, k).wait_send()
        for k in range(n_z):
            for f in range(3):
                xy_copy(h, f, k, z).wait_send()
            co_copy(h, k, z).wait_send()
        for f in range(3):
            fw_copy(h, f).wait_send()
    for j in range(n_j):
        for i in range(n_exp):
            for k in range(1, n_dp):
                ob_copy(i, j, k).wait_send()
        for k in range(1, n_z):
            zz_copy(j, k).wait_send()


def fused(hidden_in, norm_gain, expert_ids, gate_share, w_gate, w_up, w_down):
    n_dp, n_z = lax.axis_size("dp"), lax.axis_size("expert")
    tok, d_model = hidden_in.shape
    slots, units, _ = w_gate.shape
    n_exp = slots // SPLIT
    ff = SPLIT * units
    n_j = 4
    j_cols = d_model // n_j
    j_quart = j_cols // QUART
    flat = (slots * units, d_model)
    dma = pltpu.SemaphoreType.DMA
    vmem = pl.BlockSpec(memory_space=pltpu.VMEM)
    hbm = pl.BlockSpec(memory_space=pl.ANY)
    half = d_model // HALVES
    quarter = half // QUART
    gather_sems = [
        dma(dims)
        for dims in ((n_z - 1,), (3, n_z), (n_z,), (3,))
        for _ in range(2)
    ]
    return pl.pallas_call(
        functools.partial(moe_kernel, n_dp, n_z, n_exp, ff, n_j),
        out_shape=jax.ShapeDtypeStruct((tok, d_model), BF),
        in_specs=[vmem] * 4 + [hbm] * 3,
        out_specs=vmem,
        scratch_shapes=[
            pltpu.VMEM((n_dp * n_z, ROWS, quarter), BF),
            pltpu.VMEM((n_dp * n_z, ROWS, quarter + META), BF),
            pltpu.VMEM((HALVES, n_exp, n_dp * 4, half), BF),
            pltpu.VMEM((WEIGHT_SLOTS, ff, half), BF),
            pltpu.VMEM((n_exp, n_dp * 4, ff), F32),
            pltpu.VMEM((n_exp, n_dp * 4, ff), F32),
            pltpu.VMEM((n_dp * 4, ff), BF),
            pltpu.VMEM((HALVES, ROWS, quarter + META), F32),
            pltpu.VMEM((n_exp, n_j, n_dp, ROWS, j_quart), BF),
            pltpu.VMEM((n_exp, n_j, n_dp, ROWS, j_quart), BF),
            pltpu.VMEM((n_j, n_z, ROWS, j_quart), BF),
            pltpu.VMEM((n_j, n_z, ROWS, j_quart), BF),
            pltpu.VMEM((n_j, n_z, ROWS, j_quart), F32),
            pltpu.VMEM((n_j, ROWS, j_quart), F32),
            pltpu.VMEM((n_exp, n_z * ROWS, n_dp * ROWS), BF),
            dma((WEIGHT_SLOTS,)),
            *gather_sems,
            *gather_sems,
            dma((n_exp, n_j, n_dp - 1)), dma((n_exp, n_j, n_dp - 1)),
            dma((n_j, n_z - 1)), dma((n_j, n_z - 1)),
        ],
        compiler_params=pltpu.CompilerParams(
            collective_id=0, has_side_effects=True, vmem_limit_bytes=60 * 1024 * 1024
        ),
        cost_estimate=pl.CostEstimate(
            flops=6 * slots * units * d_model * n_dp * 4,
            bytes_accessed=6 * slots * units * d_model,
            transcendentals=slots * units * n_dp * 4,
        ),
        name="routed_experts",
    )(
        hidden_in, norm_gain, expert_ids, gate_share,
        w_gate.reshape(flat), w_up.reshape(flat), w_down.reshape(flat),
    )


def by_parts(hidden_in, norm_gain, expert_ids, gate_share, w_gate, w_up, w_down):
    dp_count = lax.axis_size("dp")
    col_count = lax.axis_size("expert")
    row_index = lax.axis_index("dp")
    column = lax.axis_index("expert")
    tok_dev = hidden_in.shape[0]
    model_width = hidden_in.shape[1]
    slot_dev = w_gate.shape[0]
    block_units = w_gate.shape[1]
    experts_row = EXPERTS // dp_count
    per_dev = max(1, slot_dev // SPLIT)
    runs_dev = slot_dev // per_dev
    capacity = tok_dev * col_count // 4
    resid = hidden_in.astype(jnp.float32)
    inv_rms = lax.rsqrt(jnp.mean(resid * resid, axis=1, keepdims=True) + 1e-06)
    normed = (resid * inv_rms * norm_gain.astype(jnp.float32)[None, :]).astype(jnp.bfloat16)
    row_x, row_share, row_ids = (
        lax.all_gather(normed, "expert", axis=0, tiled=True),
        lax.all_gather(gate_share, "expert", axis=0, tiled=True),
        lax.all_gather(expert_ids, "expert", axis=0, tiled=True),
    )
    tok_row = row_x.shape[0]
    flat_ids = row_ids.reshape(-1)
    onehot = (flat_ids[:, None] == jnp.arange(EXPERTS, dtype=jnp.int32)[None, :]).astype(jnp.int32)
    order_pos = jnp.sum((jnp.cumsum(onehot, axis=0) - onehot) * onehot, axis=1)
    slot_keys = (flat_ids * capacity + order_pos).reshape(tok_row, row_ids.shape[1])
    dest_rows = jnp.arange(dp_count, dtype=jnp.int32)[:, None]
    held = (dest_rows * col_count + column) * slot_dev // SPLIT + jnp.arange(
        per_dev, dtype=jnp.int32
    )[None, :]
    targets = held[:, :, None] * capacity + jnp.arange(capacity, dtype=jnp.int32)[None, None, :]
    matches = slot_keys[None, None, None, :, :] == targets[:, :, :, None, None]
    share_f = row_share.astype(jnp.float32)[None, None, None, :, :]
    weighted = jnp.sum(jnp.where(matches, share_f, 0.0), axis=4).astype(jnp.bfloat16)
    gate_w = w_gate.reshape(per_dev, runs_dev, block_units, model_width)
    up_w = w_up.reshape(per_dev, runs_dev, block_units, model_width)
    down_w = w_down.reshape(per_dev, runs_dev, block_units, model_width)
    part_rows = capacity // col_count
    row_experts = dest_rows * experts_row + jnp.arange(experts_row, dtype=jnp.int32)[None, :]
    section_targets = (
        row_experts[:, :, None] * capacity
        + column * part_rows
        + jnp.arange(part_rows, dtype=jnp.int32)[None, None, :]
    )
    section_hits = jnp.any(
        slot_keys[None, None, None, :, :] == section_targets[:, :, :, None, None], axis=4
    )
    section_blocks = jnp.einsum(
        "qmst,td->qmsd",
        section_hits.astype(jnp.bfloat16),
        row_x,
        preferred_element_type=jnp.float32,
    ).astype(jnp.bfloat16)
    landed = lax.all_to_all(section_blocks, "dp", split_axis=0, concat_axis=0, tiled=True)
    own_first = (row_index * col_count + column) * slot_dev // SPLIT - row_index * experts_row
    own_rows = lax.dynamic_slice_in_dim(
        lax.all_gather(landed, "expert", axis=2, tiled=True), own_first, per_dev, 1
    )
    gate_vals = jnp.einsum("qisd,igfd->qisgf", own_rows, gate_w, preferred_element_type=jnp.float32)
    up_vals = jnp.einsum("qisd,igfd->qisgf", own_rows, up_w, preferred_element_type=jnp.float32)
    activated = (jax.nn.silu(gate_vals) * up_vals).astype(jnp.bfloat16)
    projected = jnp.einsum(
        "qisgf,igfd->qisd", activated, down_w, preferred_element_type=jnp.float32
    )
    partial_value = projected.astype(jnp.bfloat16)
    returned = lax.all_to_all(partial_value, "dp", split_axis=0, concat_axis=0, tiled=True)
    routed = lax.psum_scatter(
        jnp.einsum("qist,qisd->td", weighted, returned, preferred_element_type=jnp.float32).astype(
            jnp.bfloat16
        ),
        "expert",
        scatter_dimension=0,
        tiled=True,
    ).astype(jnp.float32)
    return (resid + routed).astype(jnp.bfloat16)


def body(hidden_in, norm_gain, expert_ids, gate_share, w_gate, w_up, w_down):
    args = (hidden_in, norm_gain, expert_ids, gate_share, w_gate, w_up, w_down)
    whole_experts = w_gate.shape[0] % SPLIT == 0
    if whole_experts and lax.axis_size("dp") == 8 and lax.axis_size("expert") == 4:
        return fused(*args)
    return by_parts(*args)


def solution(mesh):
    placed = (
        P(("dp", "expert"), None),
        P(),
        P(("dp", "expert"), None),
        P(("dp", "expert"), None),
        P(("dp", "expert"), None, None),
        P(("dp", "expert"), None, None),
        P(("dp", "expert"), None, None),
    )
    return jax.shard_map(
        body, mesh=mesh, in_specs=placed, out_specs=P(("dp", "expert"), None), check_vma=False
    )
```

```python
import functools

import jax
import jax.numpy as jnp
from jax import lax
from jax.experimental import pallas as pl
from jax.experimental.pallas import tpu as pltpu
from jax.sharding import PartitionSpec as P

EXPERTS = 64
SPLIT = 8

ROWS = 16
QUART = 4
META = 128
WEIGHT_SLOTS = 8
HALVES = 2
MESH = pl.DeviceIdType.MESH
BF = jnp.bfloat16
F32 = jnp.float32


def iota(shape, dim):
    return lax.broadcasted_iota(jnp.int32, shape, dim)


def dot(a, b):
    return jnp.dot(a, b, preferred_element_type=F32)


def dot_nt(a, b):
    return lax.dot_general(a, b, (((1,), (1,)), ((), ())), preferred_element_type=F32)


def tok_of(r):
    return (r // ROWS) % QUART * 4 + r % 4


def quarter_of(r):
    return r % ROWS // 4


def moe_kernel(
    n_dp, n_z, n_exp, ff, n_j,
    hid_ref, gain_ref, ids_ref, share_ref, wg, wu, wd,
    out_ref,
    buf, meta_buf, xs, wbuf, acc_g, acc_u, act, pay, ob_send, ob_recv, z_send, z_recv, z_own,
    fin, wmat,
    w_sem,
    zs_s, zs_r, xy_s, xy_r, co_s, co_r, fw_s, fw_r,
    mz_s, mz_r, mxy_s, mxy_r, mco_s, mco_r, mfw_s, mfw_r,
    ob_s, ob_r, zz_s, zz_r,
):
    dp = lax.axis_index("dp")
    z = lax.axis_index("expert")
    d_model = hid_ref.shape[1]
    half = d_model // HALVES
    quarter = half // QUART
    j_cols = d_model // n_j
    j_quart = j_cols // QUART
    cap_rows = n_dp * 4
    n_rows = n_dp * n_z * ROWS

    n_head = 2 * n_exp

    def w_copy(ref, i, h, n):
        slot = lax.rem(n, WEIGHT_SLOTS)
        return pltpu.make_async_copy(
            ref.at[
                pl.ds(pl.multiple_of(i * ff, ff), ff),
                pl.ds(pl.multiple_of(h * half, half), half),
            ],
            wbuf.at[slot],
            w_sem.at[slot],
        )

    def chunk(n):
        if n < n_head:
            return w_copy((wg, wu)[n % 2], jnp.int32(n // 2), 0, jnp.int32(n))
        i, at = divmod(n - n_head, 4)
        ref, h = ((wg, 1), (wu, 1), (wd, 0), (wd, 1))[at]
        return w_copy(ref, jnp.int32(i), h, jnp.int32(n))

    n_chunks = n_head + 4 * n_exp
    first_copies = iter([chunk(n) for n in range(min(WEIGHT_SLOTS, n_chunks))])

    def stream(count):
        for _, copy in zip(range(count), first_copies):
            copy.start()

    stream(2)

    core = lax.rem(dp, 2)
    xc = lax.rem(lax.div(dp, 2), 2)
    yc = lax.div(dp, 4)
    flip_c = 1 - 2 * core
    flip_x = 2 - 4 * xc
    flip_y = 4 - 8 * yc
    sib = dp + flip_c
    flips = (flip_x, flip_y, flip_x + flip_y)
    barrier = pltpu.get_barrier_semaphore()
    for k in range(1, n_dp):
        pl.semaphore_signal(
            barrier, inc=1, device_id=(lax.rem(dp + k, n_dp), z), device_id_type=MESH
        )
    for k in range(1, n_z):
        pl.semaphore_signal(
            barrier, inc=1, device_id=(dp, lax.rem(z + k, n_z)), device_id_type=MESH
        )

    resid = hid_ref[...].astype(F32)
    inv_rms = lax.rsqrt(jnp.mean(resid * resid, axis=1, keepdims=True) + 1e-06)
    normed = resid * inv_rms * gain_ref[...].astype(F32).reshape(1, d_model)
    put = iota((8, META), 1) - iota((8, META), 0)
    meta = dot(ids_ref[...].astype(F32).astype(BF), (put == 0).astype(F32).astype(BF)) + dot(
        share_ref[...], (put == 8).astype(F32).astype(BF)
    )
    me = dp * n_z + z
    for h in range(HALVES):
        for q in range(QUART):
            at = h * half + q * quarter
            pay[h, 4 * q : 4 * q + 4, 0:quarter] = normed[:, at : at + quarter]
            if h == 0:
                pay[0, 4 * q : 4 * q + 4, quarter : quarter + META] = meta
    meta_buf[me] = pay[0].astype(BF)
    buf[me] = pay[1, :, 0:quarter].astype(BF)

    pl.semaphore_wait(barrier, n_dp - 1 + n_z - 1)

    def remote(src, dst, s, r, to):
        return pltpu.make_async_remote_copy(
            src_ref=src, dst_ref=dst, send_sem=s, recv_sem=r, device_id=to, device_id_type=MESH
        )

    held = (meta_buf, buf)
    sems = (
        (mz_s, mz_r, mxy_s, mxy_r, mco_s, mco_r, mfw_s, mfw_r),
        (zs_s, zs_r, xy_s, xy_r, co_s, co_r, fw_s, fw_r),
    )

    def z_copy(h, k):
        blk = held[h].at[me]
        s, r = sems[h][0:2]
        return remote(blk, blk, s.at[k - 1], r.at[k - 1], (dp, lax.rem(z + k, n_z)))

    def xy_copy(h, f, k, zb):
        blk = held[h].at[dp * n_z + zb]
        s, r = sems[h][2:4]
        return remote(blk, blk, s.at[f, k], r.at[f, k], (dp + flips[f], z))

    def co_copy(h, k, zb):
        blk = held[h].at[dp * n_z + zb]
        s, r = sems[h][4:6]
        return remote(blk, blk, s.at[k], r.at[k], (sib, z))

    def fw_copy(h, f):
        blk = held[h].at[pl.ds((dp + flips[f]) * n_z, n_z)]
        s, r = sems[h][6:8]
        return remote(blk, blk, s.at[f], r.at[f], (sib, z))

    def forward(h):
        for f in range(3):
            for k in range(n_z):
                xy_copy(h, f, k, z).wait_recv()
            fw_copy(h, f).start()

    def arrived(h):
        for k in range(n_z):
            co_copy(h, k, z).wait_recv()
        for f in range(3):
            fw_copy(h, f).wait_recv()

    for h in range(HALVES):
        for k in range(1, n_z):
            z_copy(h, k).start()
    for h in range(HALVES):
        for k in range(n_z):
            zb = lax.rem(z + n_z - k, n_z)
            if k > 0:
                z_copy(h, k).wait_recv()
            for f in range(3):
                xy_copy(h, f, k, zb).start()
            co_copy(h, k, zb).start()
        stream(2)

    tr, tc = iota((n_rows, 1), 0), iota((1, n_rows), 1)
    before = (
        (tr // (n_z * ROWS) == tc // (n_z * ROWS))
        & (quarter_of(tr) == 0)
        & (tok_of(tr) < tok_of(tc))
    )
    before = before.astype(F32).astype(BF)

    forward(0)
    stream(WEIGHT_SLOTS)

    grp = n_z * ROWS
    meta_g = (
        meta_buf[pl.ds(dp * n_z, n_z), :, quarter : quarter + META].reshape(grp, META).astype(F32)
    )
    gr, gc = iota((grp, 1), 0), iota((1, grp), 1)
    before_g = ((quarter_of(gc) == 0) & (tok_of(gc) < tok_of(gr))).astype(F32).astype(BF)
    lanes = n_dp * ROWS
    lc = iota((1, lanes), 1)
    lane_first = ((lc // ROWS * n_z + z) * n_exp).astype(F32)
    same_q = quarter_of(gr) == quarter_of(lc)
    lane_slot = (lc % 4).astype(F32)
    for i in range(n_exp):
        hits = jnp.zeros((grp, lanes), F32)
        shares = jnp.zeros((grp, lanes), F32)
        for k in range(8):
            match = meta_g[:, k : k + 1] == lane_first + i
            hits = hits + match.astype(F32)
            shares = shares + jnp.where(match, meta_g[:, 8 + k : 9 + k], 0.0)
        rank = dot(before_g, hits.astype(BF))
        keep = (hits > 0) & (rank == lane_slot) & same_q
        wmat[i] = jnp.where(keep, shares, 0.0).astype(BF)

    arrived(0)

    meta_all = meta_buf[:, :, quarter : quarter + META].reshape(n_rows, META)
    pick = (iota((16, META), 0) == iota((16, META), 1)).astype(F32).astype(BF)
    meta_t = dot_nt(pick, meta_all)
    ids_t = meta_t[0:8]
    first = (me * n_exp).astype(F32)
    lane_q = quarter_of(tc)
    group = (tc // (n_z * ROWS) * 4).astype(F32)
    slot_iota = iota((n_exp * cap_rows, 1), 0)
    key = jnp.full((1, n_rows), -1.0, F32)
    for i in range(n_exp):
        hit = jnp.sum((ids_t == first + i).astype(F32), axis=0, keepdims=True)
        rank = dot(jnp.broadcast_to(hit, (8, n_rows)).astype(BF), before)[0:1]
        own_key = jnp.where(hit > 0, group + rank + i * cap_rows, -1.0)
        key = jnp.where(slot_iota // cap_rows == i, own_key, key)
    chosen = slot_iota.astype(F32) == key

    def pick_rows(h):
        for q in range(QUART):
            sel = (chosen & (lane_q == q)).astype(F32).astype(BF)
            rows = dot(sel, held[h][:, :, 0:quarter].reshape(n_rows, quarter))
            for i in range(n_exp):
                xs[h, i, q * quarter : (q + 1) * quarter, :] = jnp.transpose(
                    rows[i * cap_rows : (i + 1) * cap_rows]
                ).astype(BF)

    pick_rows(0)

    def ob_copy(i, j, k):
        to = lax.rem(dp + k, n_dp)
        return remote(
            ob_send.at[i, j, to], ob_recv.at[i, j, dp], ob_s.at[i, j, k - 1],
            ob_r.at[i, j, k - 1], (to, z),
        )

    pr, pc = iota((lanes, 1), 0), iota((1, cap_rows), 1)
    same_slot = pr // ROWS * 4 + pr % 4 == pc
    spread = [
        (same_slot & (quarter_of(pr) == q)).astype(F32).astype(BF) for q in range(QUART)
    ]

    def head(i, carry):
        w_copy(wg, i, 0, 2 * i).wait()
        acc_g[i] = dot(wbuf[2 * i], xs[0, i])
        w_copy(wu, i, 0, 2 * i + 1).wait()
        acc_u[i] = dot(wbuf[2 * i + 1], xs[0, i])

        @pl.when(i == 0)
        def _():
            chunk(WEIGHT_SLOTS).start()
            chunk(WEIGHT_SLOTS + 1).start()
            forward(1)

        return carry

    lax.fori_loop(0, n_exp, head, 0)
    chunk(WEIGHT_SLOTS + 2).start()
    chunk(WEIGHT_SLOTS + 3).start()
    arrived(1)
    pick_rows(1)

    def expert(i, carry):
        n = n_head + 4 * i
        w_copy(wg, i, 1, n).wait()
        gate = acc_g[i] + dot(wbuf[lax.rem(n, WEIGHT_SLOTS)], xs[1, i])
        gate = gate / (1.0 + jnp.exp(-gate))
        w_copy(wu, i, 1, n + 1).wait()
        up = acc_u[i] + dot(wbuf[lax.rem(n + 1, WEIGHT_SLOTS)], xs[1, i])
        act[...] = jnp.transpose(gate * up).astype(BF)

        def d_step(j, carry):
            h = j // (n_j // HALVES)
            slot = lax.rem(n + 2 + h, WEIGHT_SLOTS)
            col = pl.multiple_of((j - h * (n_j // HALVES)) * j_cols, j_cols)

            @pl.when(col == 0)
            def _():
                w_copy(wd, i, h, n + 2 + h).wait()

            total = dot(act[...], wbuf[slot, :, pl.ds(col, j_cols)]).astype(BF)
            rows = dot(spread[0], total[:, 0:j_quart])
            for q in range(1, QUART):
                rows = rows + dot(spread[q], total[:, q * j_quart : (q + 1) * j_quart])
            ob_send[i, j] = rows.astype(BF).reshape(n_dp, ROWS, j_quart)
            for k in range(1, n_dp):
                ob_copy(i, j, k).start()
            ob_recv[i, j, dp] = ob_send[i, j, dp]
            return carry

        lax.fori_loop(0, n_j, d_step, 0)
        return carry

    lax.fori_loop(0, n_exp, expert, 0)

    def zz_copy(j, k):
        to = lax.rem(z + k, n_z)
        return remote(
            z_send.at[j, to], z_recv.at[j, z], zz_s.at[j, k - 1], zz_r.at[j, k - 1], (dp, to)
        )

    for j in range(n_j):
        part = jnp.zeros((grp, j_quart), F32)
        for i in range(n_exp):
            for k in range(1, n_dp):
                ob_copy(i, j, k).wait_recv()
            part = part + dot(wmat[i], ob_recv[i, j].reshape(lanes, j_quart))
        z_send[j] = part.astype(BF).reshape(n_z, ROWS, j_quart)
        z_own[j] = part.reshape(n_z, ROWS, j_quart)
        for k in range(1, n_z):
            zz_copy(j, k).start()
    for j in range(n_j):
        total = z_own[j, z]
        for k in range(1, n_z):
            zz_copy(j, k).wait_recv()
            total = total + z_recv[j, lax.rem(z + n_z - k, n_z)].astype(F32)
        fin[j] = total
        for q in range(QUART):
            at = j * j_cols + q * j_quart
            out_ref[:, at : at + j_quart] = (
                hid_ref[:, at : at + j_quart].astype(F32) + fin[j, 4 * q : 4 * q + 4, :]
            ).astype(BF)

    for h in range(HALVES):
        for k in range(1, n_z):
            z_copy(h, k).wait_send()
        for k in range(n_z):
            for f in range(3):
                xy_copy(h, f, k, z).wait_send()
            co_copy(h, k, z).wait_send()
        for f in range(3):
            fw_copy(h, f).wait_send()
    for j in range(n_j):
        for i in range(n_exp):
            for k in range(1, n_dp):
                ob_copy(i, j, k).wait_send()
        for k in range(1, n_z):
            zz_copy(j, k).wait_send()


def fused(hidden_in, norm_gain, expert_ids, gate_share, w_gate, w_up, w_down):
    n_dp, n_z = lax.axis_size("dp"), lax.axis_size("expert")
    tok, d_model = hidden_in.shape
    slots, units, _ = w_gate.shape
    n_exp = slots // SPLIT
    ff = SPLIT * units
    n_j = 4
    j_cols = d_model // n_j
    j_quart = j_cols // QUART
    flat = (slots * units, d_model)
    dma = pltpu.SemaphoreType.DMA
    vmem = pl.BlockSpec(memory_space=pltpu.VMEM)
    hbm = pl.BlockSpec(memory_space=pl.ANY)
    half = d_model // HALVES
    quarter = half // QUART
    gather_sems = [
        dma(dims)
        for dims in ((n_z - 1,), (3, n_z), (n_z,), (3,))
        for _ in range(2)
    ]
    return pl.pallas_call(
        functools.partial(moe_kernel, n_dp, n_z, n_exp, ff, n_j),
        out_shape=jax.ShapeDtypeStruct((tok, d_model), BF),
        in_specs=[vmem] * 4 + [hbm] * 3,
        out_specs=vmem,
        scratch_shapes=[
            pltpu.VMEM((n_dp * n_z, ROWS, quarter), BF),
            pltpu.VMEM((n_dp * n_z, ROWS, quarter + META), BF),
            pltpu.VMEM((HALVES, n_exp, half, n_dp * 4), BF),
            pltpu.VMEM((WEIGHT_SLOTS, ff, half), BF),
            pltpu.VMEM((n_exp, ff, n_dp * 4), F32),
            pltpu.VMEM((n_exp, ff, n_dp * 4), F32),
            pltpu.VMEM((n_dp * 4, ff), BF),
            pltpu.VMEM((HALVES, ROWS, quarter + META), F32),
            pltpu.VMEM((n_exp, n_j, n_dp, ROWS, j_quart), BF),
            pltpu.VMEM((n_exp, n_j, n_dp, ROWS, j_quart), BF),
            pltpu.VMEM((n_j, n_z, ROWS, j_quart), BF),
            pltpu.VMEM((n_j, n_z, ROWS, j_quart), BF),
            pltpu.VMEM((n_j, n_z, ROWS, j_quart), F32),
            pltpu.VMEM((n_j, ROWS, j_quart), F32),
            pltpu.VMEM((n_exp, n_z * ROWS, n_dp * ROWS), BF),
            dma((WEIGHT_SLOTS,)),
            *gather_sems,
            *gather_sems,
            dma((n_exp, n_j, n_dp - 1)), dma((n_exp, n_j, n_dp - 1)),
            dma((n_j, n_z - 1)), dma((n_j, n_z - 1)),
        ],
        compiler_params=pltpu.CompilerParams(
            collective_id=0, has_side_effects=True, vmem_limit_bytes=60 * 1024 * 1024
        ),
        cost_estimate=pl.CostEstimate(
            flops=6 * slots * units * d_model * n_dp * 4,
            bytes_accessed=6 * slots * units * d_model,
            transcendentals=slots * units * n_dp * 4,
        ),
        name="routed_experts",
    )(
        hidden_in, norm_gain, expert_ids, gate_share,
        w_gate.reshape(flat), w_up.reshape(flat), w_down.reshape(flat),
    )


def by_parts(hidden_in, norm_gain, expert_ids, gate_share, w_gate, w_up, w_down):
    dp_count = lax.axis_size("dp")
    col_count = lax.axis_size("expert")
    row_index = lax.axis_index("dp")
    column = lax.axis_index("expert")
    tok_dev = hidden_in.shape[0]
    model_width = hidden_in.shape[1]
    slot_dev = w_gate.shape[0]
    block_units = w_gate.shape[1]
    experts_row = EXPERTS // dp_count
    per_dev = max(1, slot_dev // SPLIT)
    runs_dev = slot_dev // per_dev
    capacity = tok_dev * col_count // 4
    resid = hidden_in.astype(jnp.float32)
    inv_rms = lax.rsqrt(jnp.mean(resid * resid, axis=1, keepdims=True) + 1e-06)
    normed = (resid * inv_rms * norm_gain.astype(jnp.float32)[None, :]).astype(jnp.bfloat16)
    row_x, row_share, row_ids = (
        lax.all_gather(normed, "expert", axis=0, tiled=True),
        lax.all_gather(gate_share, "expert", axis=0, tiled=True),
        lax.all_gather(expert_ids, "expert", axis=0, tiled=True),
    )
    tok_row = row_x.shape[0]
    flat_ids = row_ids.reshape(-1)
    onehot = (flat_ids[:, None] == jnp.arange(EXPERTS, dtype=jnp.int32)[None, :]).astype(jnp.int32)
    order_pos = jnp.sum((jnp.cumsum(onehot, axis=0) - onehot) * onehot, axis=1)
    slot_keys = (flat_ids * capacity + order_pos).reshape(tok_row, row_ids.shape[1])
    dest_rows = jnp.arange(dp_count, dtype=jnp.int32)[:, None]
    held = (dest_rows * col_count + column) * slot_dev // SPLIT + jnp.arange(
        per_dev, dtype=jnp.int32
    )[None, :]
    targets = held[:, :, None] * capacity + jnp.arange(capacity, dtype=jnp.int32)[None, None, :]
    matches = slot_keys[None, None, None, :, :] == targets[:, :, :, None, None]
    share_f = row_share.astype(jnp.float32)[None, None, None, :, :]
    weighted = jnp.sum(jnp.where(matches, share_f, 0.0), axis=4).astype(jnp.bfloat16)
    gate_w = w_gate.reshape(per_dev, runs_dev, block_units, model_width)
    up_w = w_up.reshape(per_dev, runs_dev, block_units, model_width)
    down_w = w_down.reshape(per_dev, runs_dev, block_units, model_width)
    part_rows = capacity // col_count
    row_experts = dest_rows * experts_row + jnp.arange(experts_row, dtype=jnp.int32)[None, :]
    section_targets = (
        row_experts[:, :, None] * capacity
        + column * part_rows
        + jnp.arange(part_rows, dtype=jnp.int32)[None, None, :]
    )
    section_hits = jnp.any(
        slot_keys[None, None, None, :, :] == section_targets[:, :, :, None, None], axis=4
    )
    section_blocks = jnp.einsum(
        "qmst,td->qmsd",
        section_hits.astype(jnp.bfloat16),
        row_x,
        preferred_element_type=jnp.float32,
    ).astype(jnp.bfloat16)
    landed = lax.all_to_all(section_blocks, "dp", split_axis=0, concat_axis=0, tiled=True)
    own_first = (row_index * col_count + column) * slot_dev // SPLIT - row_index * experts_row
    own_rows = lax.dynamic_slice_in_dim(
        lax.all_gather(landed, "expert", axis=2, tiled=True), own_first, per_dev, 1
    )
    gate_vals = jnp.einsum("qisd,igfd->qisgf", own_rows, gate_w, preferred_element_type=jnp.float32)
    up_vals = jnp.einsum("qisd,igfd->qisgf", own_rows, up_w, preferred_element_type=jnp.float32)
    activated = (jax.nn.silu(gate_vals) * up_vals).astype(jnp.bfloat16)
    projected = jnp.einsum(
        "qisgf,igfd->qisd", activated, down_w, preferred_element_type=jnp.float32
    )
    partial_value = projected.astype(jnp.bfloat16)
    returned = lax.all_to_all(partial_value, "dp", split_axis=0, concat_axis=0, tiled=True)
    routed = lax.psum_scatter(
        jnp.einsum("qist,qisd->td", weighted, returned, preferred_element_type=jnp.float32).astype(
            jnp.bfloat16
        ),
        "expert",
        scatter_dimension=0,
        tiled=True,
    ).astype(jnp.float32)
    return (resid + routed).astype(jnp.bfloat16)


def body(hidden_in, norm_gain, expert_ids, gate_share, w_gate, w_up, w_down):
    args = (hidden_in, norm_gain, expert_ids, gate_share, w_gate, w_up, w_down)
    whole_experts = w_gate.shape[0] % SPLIT == 0
    if whole_experts and lax.axis_size("dp") == 8 and lax.axis_size("expert") == 4:
        return fused(*args)
    return by_parts(*args)


def solution(mesh):
    placed = (
        P(("dp", "expert"), None),
        P(),
        P(("dp", "expert"), None),
        P(("dp", "expert"), None),
        P(("dp", "expert"), None, None),
        P(("dp", "expert"), None, None),
        P(("dp", "expert"), None, None),
    )
    return jax.shard_map(
        body, mesh=mesh, in_specs=placed, out_specs=P(("dp", "expert"), None), check_vma=False
    )
```

```python
import functools

import jax
import jax.numpy as jnp
from jax import lax
from jax.experimental import pallas as pl
from jax.experimental.pallas import tpu as pltpu
from jax.sharding import PartitionSpec as P

EXPERTS = 64
SPLIT = 8

ROWS = 16
QUART = 4
META = 128
WEIGHT_SLOTS = 9
TILE = 256
HALVES = 2
MESH = pl.DeviceIdType.MESH
BF = jnp.bfloat16
F32 = jnp.float32


def iota(shape, dim):
    return lax.broadcasted_iota(jnp.int32, shape, dim)


def dot(a, b):
    return jnp.dot(a, b, preferred_element_type=F32)


def dot_nt(a, b):
    return lax.dot_general(a, b, (((1,), (1,)), ((), ())), preferred_element_type=F32)


def tok_of(r):
    return (r // ROWS) % QUART * 4 + r % 4


def quarter_of(r):
    return r % ROWS // 4


def moe_kernel(
    n_dp, n_z, n_exp, ff, n_j,
    hid_ref, gain_ref, ids_ref, share_ref, wg, wu, wd,
    out_ref,
    buf, meta_buf, xs, wbuf, acc_g, acc_u, act, pay, ob_send, ob_recv, z_send, z_recv, z_own,
    fin, wmat,
    w_sem,
    zs_s, zs_r, xy_s, xy_r, co_s, co_r, fw_s, fw_r,
    mz_s, mz_r, mxy_s, mxy_r, mco_s, mco_r, mfw_s, mfw_r,
    ob_s, ob_r, zz_s, zz_r,
):
    dp = lax.axis_index("dp")
    z = lax.axis_index("expert")
    d_model = hid_ref.shape[1]
    half = d_model // HALVES
    quarter = half // QUART
    j_cols = d_model // n_j
    j_quart = j_cols // QUART
    cap_rows = n_dp * 4
    n_rows = n_dp * n_z * ROWS

    n_head = 2 * n_exp

    def w_copy(ref, i, h, n):
        slot = lax.rem(n, WEIGHT_SLOTS)
        return pltpu.make_async_copy(
            ref.at[
                pl.ds(pl.multiple_of(i * ff, ff), ff),
                pl.ds(pl.multiple_of(h * half, half), half),
            ],
            wbuf.at[slot],
            w_sem.at[slot],
        )

    def chunk(n):
        if n < n_head:
            return w_copy((wg, wu)[n % 2], jnp.int32(n // 2), 0, jnp.int32(n))
        i, at = divmod(n - n_head, 4)
        ref, h = ((wg, 1), (wu, 1), (wd, 0), (wd, 1))[at]
        return w_copy(ref, jnp.int32(i), h, jnp.int32(n))

    n_chunks = n_head + 4 * n_exp
    first_copies = iter([chunk(n) for n in range(min(WEIGHT_SLOTS, n_chunks))])

    def stream(count):
        for _, copy in zip(range(count), first_copies):
            copy.start()

    stream(2)

    core = lax.rem(dp, 2)
    xc = lax.rem(lax.div(dp, 2), 2)
    yc = lax.div(dp, 4)
    flip_c = 1 - 2 * core
    flip_x = 2 - 4 * xc
    flip_y = 4 - 8 * yc
    sib = dp + flip_c
    flips = (flip_x, flip_y, flip_x + flip_y)
    barrier = pltpu.get_barrier_semaphore()
    for k in range(1, n_dp):
        pl.semaphore_signal(
            barrier, inc=1, device_id=(lax.rem(dp + k, n_dp), z), device_id_type=MESH
        )
    for k in range(1, n_z):
        pl.semaphore_signal(
            barrier, inc=1, device_id=(dp, lax.rem(z + k, n_z)), device_id_type=MESH
        )

    resid = hid_ref[...].astype(F32)
    inv_rms = lax.rsqrt(jnp.mean(resid * resid, axis=1, keepdims=True) + 1e-06)
    normed = resid * inv_rms * gain_ref[...].astype(F32).reshape(1, d_model)
    put = iota((8, META), 1) - iota((8, META), 0)
    meta = dot(ids_ref[...].astype(F32).astype(BF), (put == 0).astype(F32).astype(BF)) + dot(
        share_ref[...], (put == 8).astype(F32).astype(BF)
    )
    me = dp * n_z + z
    for h in range(HALVES):
        for q in range(QUART):
            at = h * half + q * quarter
            pay[h, 4 * q : 4 * q + 4, 0:quarter] = normed[:, at : at + quarter]
            if h == 0:
                pay[0, 4 * q : 4 * q + 4, quarter : quarter + META] = meta
    meta_buf[me] = pay[0].astype(BF)
    buf[me] = pay[1, :, 0:quarter].astype(BF)

    pl.semaphore_wait(barrier, n_dp - 1 + n_z - 1)

    def remote(src, dst, s, r, to):
        return pltpu.make_async_remote_copy(
            src_ref=src, dst_ref=dst, send_sem=s, recv_sem=r, device_id=to, device_id_type=MESH
        )

    held = (meta_buf, buf)
    sems = (
        (mz_s, mz_r, mxy_s, mxy_r, mco_s, mco_r, mfw_s, mfw_r),
        (zs_s, zs_r, xy_s, xy_r, co_s, co_r, fw_s, fw_r),
    )

    def z_copy(h, k):
        blk = held[h].at[me]
        s, r = sems[h][0:2]
        return remote(blk, blk, s.at[k - 1], r.at[k - 1], (dp, lax.rem(z + k, n_z)))

    def xy_copy(h, f, k, zb):
        blk = held[h].at[dp * n_z + zb]
        s, r = sems[h][2:4]
        return remote(blk, blk, s.at[f, k], r.at[f, k], (dp + flips[f], z))

    def co_copy(h, k, zb):
        blk = held[h].at[dp * n_z + zb]
        s, r = sems[h][4:6]
        return remote(blk, blk, s.at[k], r.at[k], (sib, z))

    def fw_copy(h, f):
        blk = held[h].at[pl.ds((dp + flips[f]) * n_z, n_z)]
        s, r = sems[h][6:8]
        return remote(blk, blk, s.at[f], r.at[f], (sib, z))

    def forward(h):
        for f in range(3):
            for k in range(n_z):
                xy_copy(h, f, k, z).wait_recv()
            fw_copy(h, f).start()

    def arrived(h):
        for k in range(n_z):
            co_copy(h, k, z).wait_recv()
        for f in range(3):
            fw_copy(h, f).wait_recv()

    for h in range(HALVES):
        for k in range(1, n_z):
            z_copy(h, k).start()
    for h in range(HALVES):
        for k in range(n_z):
            zb = lax.rem(z + n_z - k, n_z)
            if k > 0:
                z_copy(h, k).wait_recv()
            for f in range(3):
                xy_copy(h, f, k, zb).start()
            co_copy(h, k, zb).start()
        stream(2)

    tr, tc = iota((n_rows, 1), 0), iota((1, n_rows), 1)
    before = (
        (tr // (n_z * ROWS) == tc // (n_z * ROWS))
        & (quarter_of(tr) == 0)
        & (tok_of(tr) < tok_of(tc))
    )
    before = before.astype(F32).astype(BF)

    forward(0)
    stream(WEIGHT_SLOTS)

    grp = n_z * ROWS
    meta_g = (
        meta_buf[pl.ds(dp * n_z, n_z), :, quarter : quarter + META].reshape(grp, META).astype(F32)
    )
    gr, gc = iota((grp, 1), 0), iota((1, grp), 1)
    before_g = ((quarter_of(gc) == 0) & (tok_of(gc) < tok_of(gr))).astype(F32).astype(BF)
    lanes = n_dp * ROWS
    lc = iota((1, lanes), 1)
    lane_first = ((lc // ROWS * n_z + z) * n_exp).astype(F32)
    same_q = quarter_of(gr) == quarter_of(lc)
    lane_slot = (lc % 4).astype(F32)
    for i in range(n_exp):
        hits = jnp.zeros((grp, lanes), F32)
        shares = jnp.zeros((grp, lanes), F32)
        for k in range(8):
            match = meta_g[:, k : k + 1] == lane_first + i
            hits = hits + match.astype(F32)
            shares = shares + jnp.where(match, meta_g[:, 8 + k : 9 + k], 0.0)
        rank = dot(before_g, hits.astype(BF))
        keep = (hits > 0) & (rank == lane_slot) & same_q
        wmat[i] = jnp.where(keep, shares, 0.0).astype(BF)

    arrived(0)

    meta_all = meta_buf[:, :, quarter : quarter + META].reshape(n_rows, META)
    pick = (iota((16, META), 0) == iota((16, META), 1)).astype(F32).astype(BF)
    meta_t = dot_nt(pick, meta_all)
    ids_t = meta_t[0:8]
    first = (me * n_exp).astype(F32)
    lane_q = quarter_of(tc)
    group = (tc // (n_z * ROWS) * 4).astype(F32)
    slot_iota = iota((n_exp * cap_rows, 1), 0)
    key = jnp.full((1, n_rows), -1.0, F32)
    for i in range(n_exp):
        hit = jnp.sum((ids_t == first + i).astype(F32), axis=0, keepdims=True)
        rank = dot(jnp.broadcast_to(hit, (8, n_rows)).astype(BF), before)[0:1]
        own_key = jnp.where(hit > 0, group + rank + i * cap_rows, -1.0)
        key = jnp.where(slot_iota // cap_rows == i, own_key, key)
    chosen = slot_iota.astype(F32) == key

    def pick_rows(h):
        for q in range(QUART):
            sel = (chosen & (lane_q == q)).astype(F32).astype(BF)
            rows = dot(sel, held[h][:, :, 0:quarter].reshape(n_rows, quarter)).astype(BF)
            xs[h, :, :, q * quarter : (q + 1) * quarter] = rows.reshape(n_exp, cap_rows, quarter)

    pick_rows(0)

    def ob_copy(i, j, k):
        to = lax.rem(dp + k, n_dp)
        return remote(
            ob_send.at[i, j, to], ob_recv.at[i, j, dp], ob_s.at[i, j, k - 1],
            ob_r.at[i, j, k - 1], (to, z),
        )

    pr, pc = iota((lanes, 1), 0), iota((1, cap_rows), 1)
    same_slot = pr // ROWS * 4 + pr % 4 == pc
    spread = [
        (same_slot & (quarter_of(pr) == q)).astype(F32).astype(BF) for q in range(QUART)
    ]

    tiles = [slice(at, at + TILE) for at in range(0, ff, TILE)]

    def head(i, carry):
        w_copy(wg, i, 0, 2 * i).wait()
        for t in tiles:
            acc_g[i, :, t] = dot_nt(xs[0, i], wbuf[2 * i, t, :])
        w_copy(wu, i, 0, 2 * i + 1).wait()
        for t in tiles:
            acc_u[i, :, t] = dot_nt(xs[0, i], wbuf[2 * i + 1, t, :])

        @pl.when(i == 0)
        def _():
            chunk(WEIGHT_SLOTS).start()
            chunk(WEIGHT_SLOTS + 1).start()
            forward(1)

        return carry

    lax.fori_loop(0, n_exp, head, 0)
    chunk(WEIGHT_SLOTS + 2).start()
    arrived(1)
    pick_rows(1)

    def expert(i, carry):
        n = n_head + 4 * i
        w_copy(wg, i, 1, n).wait()
        slot = lax.rem(n, WEIGHT_SLOTS)
        for t in tiles:
            gate = acc_g[i, :, t] + dot_nt(xs[1, i], wbuf[slot, t, :])
            acc_g[i, :, t] = gate / (1.0 + jnp.exp(-gate))
        w_copy(wu, i, 1, n + 1).wait()
        slot_u = lax.rem(n + 1, WEIGHT_SLOTS)
        for t in tiles:
            up = acc_u[i, :, t] + dot_nt(xs[1, i], wbuf[slot_u, t, :])
            act[:, t] = (acc_g[i, :, t] * up).astype(BF)

        def d_step(j, carry):
            h = j // (n_j // HALVES)
            slot = lax.rem(n + 2 + h, WEIGHT_SLOTS)
            col = pl.multiple_of((j - h * (n_j // HALVES)) * j_cols, j_cols)

            @pl.when(col == 0)
            def _():
                w_copy(wd, i, h, n + 2 + h).wait()

            rows = jnp.zeros((lanes, j_quart), F32)
            for q in range(QUART):
                cols = pl.ds(pl.multiple_of(col + q * j_quart, j_quart), j_quart)
                total = dot(act[...], wbuf[slot, :, cols]).astype(BF)
                rows = rows + dot(spread[q], total)
            ob_send[i, j] = rows.astype(BF).reshape(n_dp, ROWS, j_quart)
            for k in range(1, n_dp):
                ob_copy(i, j, k).start()
            ob_recv[i, j, dp] = ob_send[i, j, dp]
            return carry

        lax.fori_loop(0, n_j, d_step, 0)
        return carry

    lax.fori_loop(0, n_exp, expert, 0)

    def zz_copy(j, k):
        to = lax.rem(z + k, n_z)
        return remote(
            z_send.at[j, to], z_recv.at[j, z], zz_s.at[j, k - 1], zz_r.at[j, k - 1], (dp, to)
        )

    for j in range(n_j):
        part = jnp.zeros((grp, j_quart), F32)
        for i in range(n_exp):
            for k in range(1, n_dp):
                ob_copy(i, j, k).wait_recv()
            part = part + dot(wmat[i], ob_recv[i, j].reshape(lanes, j_quart))
        z_send[j] = part.astype(BF).reshape(n_z, ROWS, j_quart)
        z_own[j] = part.reshape(n_z, ROWS, j_quart)
        for k in range(1, n_z):
            zz_copy(j, k).start()
    for j in range(n_j):
        total = z_own[j, z]
        for k in range(1, n_z):
            zz_copy(j, k).wait_recv()
            total = total + z_recv[j, lax.rem(z + n_z - k, n_z)].astype(F32)
        fin[j] = total
        for q in range(QUART):
            at = j * j_cols + q * j_quart
            out_ref[:, at : at + j_quart] = (
                hid_ref[:, at : at + j_quart].astype(F32) + fin[j, 4 * q : 4 * q + 4, :]
            ).astype(BF)

    for h in range(HALVES):
        for k in range(1, n_z):
            z_copy(h, k).wait_send()
        for k in range(n_z):
            for f in range(3):
                xy_copy(h, f, k, z).wait_send()
            co_copy(h, k, z).wait_send()
        for f in range(3):
            fw_copy(h, f).wait_send()
    for j in range(n_j):
        for i in range(n_exp):
            for k in range(1, n_dp):
                ob_copy(i, j, k).wait_send()
        for k in range(1, n_z):
            zz_copy(j, k).wait_send()


def fused(hidden_in, norm_gain, expert_ids, gate_share, w_gate, w_up, w_down):
    n_dp, n_z = lax.axis_size("dp"), lax.axis_size("expert")
    tok, d_model = hidden_in.shape
    slots, units, _ = w_gate.shape
    n_exp = slots // SPLIT
    ff = SPLIT * units
    n_j = 4
    j_cols = d_model // n_j
    j_quart = j_cols // QUART
    flat = (slots * units, d_model)
    dma = pltpu.SemaphoreType.DMA
    vmem = pl.BlockSpec(memory_space=pltpu.VMEM)
    hbm = pl.BlockSpec(memory_space=pl.ANY)
    half = d_model // HALVES
    quarter = half // QUART
    gather_sems = [
        dma(dims)
        for dims in ((n_z - 1,), (3, n_z), (n_z,), (3,))
        for _ in range(2)
    ]
    return pl.pallas_call(
        functools.partial(moe_kernel, n_dp, n_z, n_exp, ff, n_j),
        out_shape=jax.ShapeDtypeStruct((tok, d_model), BF),
        in_specs=[vmem] * 4 + [hbm] * 3,
        out_specs=vmem,
        scratch_shapes=[
            pltpu.VMEM((n_dp * n_z, ROWS, quarter), BF),
            pltpu.VMEM((n_dp * n_z, ROWS, quarter + META), BF),
            pltpu.VMEM((HALVES, n_exp, n_dp * 4, half), BF),
            pltpu.VMEM((WEIGHT_SLOTS, ff, half), BF),
            pltpu.VMEM((n_exp, n_dp * 4, ff), F32),
            pltpu.VMEM((n_exp, n_dp * 4, ff), F32),
            pltpu.VMEM((n_dp * 4, ff), BF),
            pltpu.VMEM((HALVES, ROWS, quarter + META), F32),
            pltpu.VMEM((n_exp, n_j, n_dp, ROWS, j_quart), BF),
            pltpu.VMEM((n_exp, n_j, n_dp, ROWS, j_quart), BF),
            pltpu.VMEM((n_j, n_z, ROWS, j_quart), BF),
            pltpu.VMEM((n_j, n_z, ROWS, j_quart), BF),
            pltpu.VMEM((n_j, n_z, ROWS, j_quart), F32),
            pltpu.VMEM((n_j, ROWS, j_quart), F32),
            pltpu.VMEM((n_exp, n_z * ROWS, n_dp * ROWS), BF),
            dma((WEIGHT_SLOTS,)),
            *gather_sems,
            *gather_sems,
            dma((n_exp, n_j, n_dp - 1)), dma((n_exp, n_j, n_dp - 1)),
            dma((n_j, n_z - 1)), dma((n_j, n_z - 1)),
        ],
        compiler_params=pltpu.CompilerParams(
            collective_id=0, has_side_effects=True, vmem_limit_bytes=60 * 1024 * 1024
        ),
        cost_estimate=pl.CostEstimate(
            flops=6 * slots * units * d_model * n_dp * 4,
            bytes_accessed=6 * slots * units * d_model,
            transcendentals=slots * units * n_dp * 4,
        ),
        name="routed_experts",
    )(
        hidden_in, norm_gain, expert_ids, gate_share,
        w_gate.reshape(flat), w_up.reshape(flat), w_down.reshape(flat),
    )


def by_parts(hidden_in, norm_gain, expert_ids, gate_share, w_gate, w_up, w_down):
    dp_count = lax.axis_size("dp")
    col_count = lax.axis_size("expert")
    row_index = lax.axis_index("dp")
    column = lax.axis_index("expert")
    tok_dev = hidden_in.shape[0]
    model_width = hidden_in.shape[1]
    slot_dev = w_gate.shape[0]
    block_units = w_gate.shape[1]
    experts_row = EXPERTS // dp_count
    per_dev = max(1, slot_dev // SPLIT)
    runs_dev = slot_dev // per_dev
    capacity = tok_dev * col_count // 4
    resid = hidden_in.astype(jnp.float32)
    inv_rms = lax.rsqrt(jnp.mean(resid * resid, axis=1, keepdims=True) + 1e-06)
    normed = (resid * inv_rms * norm_gain.astype(jnp.float32)[None, :]).astype(jnp.bfloat16)
    row_x, row_share, row_ids = (
        lax.all_gather(normed, "expert", axis=0, tiled=True),
        lax.all_gather(gate_share, "expert", axis=0, tiled=True),
        lax.all_gather(expert_ids, "expert", axis=0, tiled=True),
    )
    tok_row = row_x.shape[0]
    flat_ids = row_ids.reshape(-1)
    onehot = (flat_ids[:, None] == jnp.arange(EXPERTS, dtype=jnp.int32)[None, :]).astype(jnp.int32)
    order_pos = jnp.sum((jnp.cumsum(onehot, axis=0) - onehot) * onehot, axis=1)
    slot_keys = (flat_ids * capacity + order_pos).reshape(tok_row, row_ids.shape[1])
    dest_rows = jnp.arange(dp_count, dtype=jnp.int32)[:, None]
    held = (dest_rows * col_count + column) * slot_dev // SPLIT + jnp.arange(
        per_dev, dtype=jnp.int32
    )[None, :]
    targets = held[:, :, None] * capacity + jnp.arange(capacity, dtype=jnp.int32)[None, None, :]
    matches = slot_keys[None, None, None, :, :] == targets[:, :, :, None, None]
    share_f = row_share.astype(jnp.float32)[None, None, None, :, :]
    weighted = jnp.sum(jnp.where(matches, share_f, 0.0), axis=4).astype(jnp.bfloat16)
    gate_w = w_gate.reshape(per_dev, runs_dev, block_units, model_width)
    up_w = w_up.reshape(per_dev, runs_dev, block_units, model_width)
    down_w = w_down.reshape(per_dev, runs_dev, block_units, model_width)
    part_rows = capacity // col_count
    row_experts = dest_rows * experts_row + jnp.arange(experts_row, dtype=jnp.int32)[None, :]
    section_targets = (
        row_experts[:, :, None] * capacity
        + column * part_rows
        + jnp.arange(part_rows, dtype=jnp.int32)[None, None, :]
    )
    section_hits = jnp.any(
        slot_keys[None, None, None, :, :] == section_targets[:, :, :, None, None], axis=4
    )
    section_blocks = jnp.einsum(
        "qmst,td->qmsd",
        section_hits.astype(jnp.bfloat16),
        row_x,
        preferred_element_type=jnp.float32,
    ).astype(jnp.bfloat16)
    landed = lax.all_to_all(section_blocks, "dp", split_axis=0, concat_axis=0, tiled=True)
    own_first = (row_index * col_count + column) * slot_dev // SPLIT - row_index * experts_row
    own_rows = lax.dynamic_slice_in_dim(
        lax.all_gather(landed, "expert", axis=2, tiled=True), own_first, per_dev, 1
    )
    gate_vals = jnp.einsum("qisd,igfd->qisgf", own_rows, gate_w, preferred_element_type=jnp.float32)
    up_vals = jnp.einsum("qisd,igfd->qisgf", own_rows, up_w, preferred_element_type=jnp.float32)
    activated = (jax.nn.silu(gate_vals) * up_vals).astype(jnp.bfloat16)
    projected = jnp.einsum(
        "qisgf,igfd->qisd", activated, down_w, preferred_element_type=jnp.float32
    )
    partial_value = projected.astype(jnp.bfloat16)
    returned = lax.all_to_all(partial_value, "dp", split_axis=0, concat_axis=0, tiled=True)
    routed = lax.psum_scatter(
        jnp.einsum("qist,qisd->td", weighted, returned, preferred_element_type=jnp.float32).astype(
            jnp.bfloat16
        ),
        "expert",
        scatter_dimension=0,
        tiled=True,
    ).astype(jnp.float32)
    return (resid + routed).astype(jnp.bfloat16)


def body(hidden_in, norm_gain, expert_ids, gate_share, w_gate, w_up, w_down):
    args = (hidden_in, norm_gain, expert_ids, gate_share, w_gate, w_up, w_down)
    whole_experts = w_gate.shape[0] % SPLIT == 0
    if whole_experts and lax.axis_size("dp") == 8 and lax.axis_size("expert") == 4:
        return fused(*args)
    return by_parts(*args)


def solution(mesh):
    placed = (
        P(("dp", "expert"), None),
        P(),
        P(("dp", "expert"), None),
        P(("dp", "expert"), None),
        P(("dp", "expert"), None, None),
        P(("dp", "expert"), None, None),
        P(("dp", "expert"), None, None),
    )
    return jax.shard_map(
        body, mesh=mesh, in_specs=placed, out_specs=P(("dp", "expert"), None), check_vma=False
    )
```
